1024 devices in a mesh: row: 8 (over x, core), col: 128 (over y, z).
Axes of the slice: x: 4, y: 4, z: 32, core: 2. Of those that a mesh axis runs over, the one named last changes fastest.
Arguments:
- grad_out: bfloat16 [256, 53248], P('row', 'col'), may hold values from -6 to 6
- acts: bfloat16 [256, 16384], P('col', 'row'), may hold values from -6 to 6
- weight: bfloat16 [16384, 53248], P('row', 'col'), may hold values from -0.046875 to 0.046875
Outputs:
- grad_in: bfloat16 [256, 16384], P('col', 'row')
- grad_weight: bfloat16 [16384, 53248], P('row', 'col')
The draws below stay inside these ranges and needn't reach their ends.
All inputs are finite; a program needn't handle non-finite values.
Results may differ from the reference program's by a relative error of at most 0.001.
Values may be sent and summed in bfloat16 or wider, within the bound.
No kernel may reach another device: no remote copies, remote signals or barrier semaphores. Data moves between devices by JAX's collectives and lax.ppermute only.
A program may use at most 32 MiB of HBM per device.

```python
import jax
import jax.numpy as jnp
from jax import lax

D = 16384
FF = 53248
MXB = 32
TOK = 256
N_COL = 128


def draw_grad_out(key, part):
    key = jax.random.fold_in(key, 11)
    key_rows, key_cols, key_vals = jax.random.split(key, 3)
    row_scale = jnp.exp(jax.random.uniform(key_rows, (TOK, 1), jnp.float32, jnp.log(0.01), 0.0))
    col_scale = jnp.exp(jax.random.uniform(key_cols, (1, FF), jnp.float32, jnp.log(0.01), 0.0))
    values = jnp.clip(jax.random.normal(key_vals, (TOK, FF), jnp.float32), -6.0, 6.0)
    return (values * row_scale * col_scale).astype(jnp.bfloat16)


def draw_acts(key, part):
    key = jax.random.fold_in(key, 23)
    key_cols, key_vals = jax.random.split(key, 2)
    col_scale = jnp.exp(jax.random.uniform(key_cols, (1, D), jnp.float32, jnp.log(0.01), 0.0))
    values = jnp.clip(jax.random.normal(key_vals, (TOK, D), jnp.float32), -6.0, 6.0)
    return (values * col_scale).astype(jnp.bfloat16)


def block_levels(own_key, extent, shards, least, high):
    level = 1.0
    for position, blocks in shards:
        heights = jax.random.uniform(jax.random.fold_in(jax.random.fold_in(own_key, 6), position), (blocks,), jnp.float32, least / len(shards), high / len(shards))
        level = level * jnp.repeat(jnp.exp(heights), extent[position] // blocks).reshape((-1,) + (1,) * (len(extent) - 1 - position))
    return level


def noise(own_key, extent, scale, limit, pieces=(), held_as=jnp.bfloat16):
    values = jax.random.normal(own_key, extent, jnp.float32) * scale
    if len(pieces) > 0:
        values = block_levels(own_key, extent, pieces, -0.22, 0.18) * values
    return jnp.clip(values, min=-limit, max=limit).astype(held_as)


def setup_inputs(seed: int = 0) -> dict:
    streams_of = jax.random.split(jax.random.key(seed), 4)
    return {
        "grad_out": draw_grad_out(jax.random.fold_in(streams_of[3], 71), 0),
        "acts": draw_acts(jax.random.fold_in(streams_of[3], 71), 0),
        "weight": noise(streams_of[2], (D, FF), D ** -0.5, 0.046875, ((0, 8), (1, 128))),
    }


code_limit = 448.0
peak_floor = 0.25


def block_scale(peaks):
    scale = jnp.full_like(peaks, 2.0 ** -10)
    for power in range(-1, 8):
        scale = jnp.where(peaks >= 2.0 ** power, 2.0 ** (power - 8), scale)
    return scale


def grid_codes(scaled):
    clipped = jnp.clip(scaled, -code_limit, code_limit)
    magnitude = jnp.abs(clipped)
    spacing = jnp.full_like(magnitude, 2.0 ** -9)
    for power in range(-5, 9):
        spacing = jnp.where(magnitude >= 2.0 ** power, 2.0 ** (power - 3), spacing)
    return jnp.sign(clipped) * jnp.floor(magnitude / spacing + 0.5) * spacing


def requant_along_cols(values):
    height, width = values.shape
    blocks = values.astype(jnp.float32).reshape(height, width // MXB, MXB)
    peaks = jnp.maximum(jnp.max(jnp.abs(blocks), axis=2, keepdims=True), peak_floor)
    scale = block_scale(peaks)
    codes = grid_codes(blocks / scale).astype(jnp.bfloat16)
    restored = (codes.astype(jnp.float32) * scale).astype(jnp.bfloat16)
    return restored.reshape(height, width)


def requant_along_rows(values):
    height, width = values.shape
    blocks = values.astype(jnp.float32).reshape(height // MXB, MXB, width)
    peaks = jnp.maximum(jnp.max(jnp.abs(blocks), axis=1, keepdims=True), peak_floor)
    scale = block_scale(peaks)
    codes = grid_codes(blocks / scale).astype(jnp.bfloat16)
    restored = (codes.astype(jnp.float32) * scale).astype(jnp.bfloat16)
    return restored.reshape(height, width)


def reference(grad_out, acts, weight):
    grad_cols = requant_along_cols(grad_out)
    grad_toks = requant_along_rows(grad_out)
    act_toks = requant_along_rows(acts)
    grad_in = lax.dot_general(grad_cols, weight, (((1,), (1,)), ((), ())), preferred_element_type=jnp.float32).astype(jnp.bfloat16)
    panels = grad_toks.reshape(TOK, N_COL, FF // N_COL).transpose(1, 0, 2)

    def weight_tile(panel):
        return lax.dot_general(act_toks, panel, (((0,), (0,)), ((), ())), preferred_element_type=jnp.float32).astype(jnp.bfloat16)

    tiles = lax.map(weight_tile, panels)
    grad_weight = tiles.transpose(1, 0, 2).reshape(D, FF)
    return grad_in, grad_weight
```

```python
import functools

import jax
import jax.numpy as jnp
from jax import lax
from jax.experimental import pallas as pl
from jax.experimental.pallas import tpu as pltpu
from jax.sharding import Mesh
from jax.sharding import PartitionSpec as P

MXB = 32
CODE_LIMIT = 448.0
PEAK_FLOOR = 0.25
Y, ZH, ZL = 4, 8, 4
F32 = jnp.float32
BF16 = jnp.bfloat16


def block_scale(peaks):
    scale = jnp.full_like(peaks, 2.0 ** (-10))
    for power in range(-1, 8):
        scale = jnp.where(peaks >= 2.0**power, 2.0 ** (power - 8), scale)
    return scale


def requant(blocks, axis):
    peaks = jnp.maximum(jnp.max(jnp.abs(blocks), axis=axis, keepdims=True), PEAK_FLOOR)
    scale = block_scale(peaks)
    limit = CODE_LIMIT * scale
    held = jnp.minimum(jnp.maximum(blocks, -limit), limit) * (1.0 + 2.0**-12)
    wide = held * (2.0**20 + 1.0)
    normal = wide - (wide - held)
    anchor = (1.5 * 2.0**14) * scale
    small = (held + anchor) - anchor
    return jnp.where(jnp.abs(blocks) < 2.0**-6 * scale, small, normal)


def dot(a, b, dims):
    return lax.dot_general(a, b, (dims, ((), ())), preferred_element_type=F32)


def partial_kernel(y_ref, g_ref, w_ref, *out_refs):
    tok, ff = g_ref.shape
    g_t = g_ref[...].astype(F32).T
    codes_t = requant(g_t.reshape(ff // MXB, MXB, tok), 1).reshape(ff, tok).astype(BF16)
    chunk = tok // Y
    row = lax.broadcasted_iota(jnp.int32, (tok, tok), 0)
    col = lax.broadcasted_iota(jnp.int32, (tok, tok), 1)
    far, rest = row // chunk, row % chunk
    zl, zh, pair = rest // (2 * ZH), rest % (2 * ZH) // 2, rest % 2
    source = (far + y_ref[0]) % Y * chunk + (zh * ZL + zl) * 2 + pair
    order = jnp.where(col == source, 1.0, 0.0).astype(BF16)
    codes = dot(order, codes_t, ((1,), (1,))).astype(BF16)
    for d, out_ref in enumerate(out_refs):
        out_ref[...] = dot(codes[d * chunk : (d + 1) * chunk], w_ref[...], ((1,), (0,)))


def partial_sums(y, g, w_t):
    tok, ff = g.shape
    feat = w_t.shape[1]
    return pl.pallas_call(
        partial_kernel,
        out_shape=[jax.ShapeDtypeStruct((tok // Y, feat), F32)] * Y,
        in_specs=[
            pl.BlockSpec(memory_space=pltpu.SMEM),
            pl.BlockSpec(memory_space=pltpu.VMEM),
            pl.BlockSpec(memory_space=pltpu.VMEM),
        ],
        out_specs=[pl.BlockSpec(memory_space=pltpu.VMEM)] * Y,
        compiler_params=pltpu.CompilerParams(vmem_limit_bytes=32 * 2**20),
        cost_estimate=pl.CostEstimate(
            flops=2 * tok * ff * feat, bytes_accessed=2 * ff * feat + 4 * tok * feat, transcendentals=0
        ),
    )(y, g, w_t)


def weight_kernel(y_ref, g_ref, *refs):
    act_refs, out_ref, toks_ref, ahead_ref = refs[:Y], refs[Y], refs[Y + 1], refs[Y + 2]
    tok, ff = g_ref.shape
    chunk = tok // Y

    @pl.when(pl.program_id(0) == 0)
    def _():
        g = g_ref[...].astype(F32).reshape(tok // MXB, MXB, ff)
        ahead_ref[...] = requant(g, 1).reshape(tok, ff)
        parts = []
        for d in range(Y):
            start = pl.multiple_of((y_ref[0] + (Y - d)) % Y * chunk, chunk)
            parts.append(ahead_ref[pl.ds(start, chunk), :].T)
        toks_ref[...] = jnp.concatenate(parts, axis=1).astype(BF16)

    acts = []
    for act_ref in act_refs:
        a = act_ref[...].astype(F32)
        width = a.shape[1]
        acts.append(requant(a.reshape(chunk // MXB, MXB, width), 1).reshape(chunk, width).astype(BF16))
    out_ref[...] = dot(toks_ref[...], jnp.concatenate(acts, axis=0), ((1,), (0,))).astype(BF16)


def weight_grad(y, g, acts):
    tok, ff = g.shape
    feat = acts[0].shape[1]
    tile = feat // 4
    return pl.pallas_call(
        weight_kernel,
        out_shape=jax.ShapeDtypeStruct((ff, feat), BF16),
        grid=(feat // tile,),
        in_specs=[
            pl.BlockSpec(memory_space=pltpu.SMEM),
            pl.BlockSpec((tok, ff), lambda i: (0, 0)),
        ]
        + [pl.BlockSpec((tok // Y, tile), lambda i: (0, i))] * Y,
        out_specs=pl.BlockSpec((ff, tile), lambda i: (0, i)),
        scratch_shapes=[pltpu.VMEM((ff, tok), BF16), pltpu.VMEM((tok, ff), F32)],
        compiler_params=pltpu.CompilerParams(vmem_limit_bytes=32 * 2**20),
        cost_estimate=pl.CostEstimate(
            flops=2 * tok * ff * feat + 20 * tok * feat,
            bytes_accessed=2 * ff * feat + 2 * tok * feat,
            transcendentals=0,
        ),
    )(y, g, *acts)


def along_y(x, distance):
    return lax.ppermute(x, "y", [(k, (k + distance) % Y) for k in range(Y)])


def local(grad_out, acts, weight):
    y = lax.axis_index("y").astype(jnp.int32).reshape(1)
    z = ZH * ZL
    rows, feat = acts.shape

    copies = jnp.broadcast_to(acts[None], (z, rows, feat))
    z_acts = lax.all_to_all(copies, ("zh", "zl"), 0, 0).reshape(z * rows, feat)
    g = lax.all_gather(grad_out, ("x", "core"), axis=0, tiled=True)

    sums = partial_sums(y, g, weight.T)
    arrived = [along_y(sums[d], d) for d in (2, 1, 3)]
    total = sums[0] + arrived[0] + arrived[1] + arrived[2]
    total = lax.psum_scatter(total, "zl", scatter_dimension=0, tiled=True)

    all_acts = [z_acts] + [along_y(z_acts, d) for d in (1, 2, 3)]

    parts = lax.all_to_all(total.reshape(ZH, rows, feat), "zh", 0, 0)
    grad_weight = weight_grad(y, g, all_acts).T
    grad_in = jnp.sum(parts, axis=0).astype(BF16)
    return grad_in, grad_weight


def solution(mesh):
    fine = Mesh(mesh.devices.reshape(4, 2, Y, ZH, ZL), ("x", "core", "y", "zh", "zl"))
    row, col = ("x", "core"), ("y", "zh", "zl")
    return jax.shard_map(
        local,
        mesh=fine,
        in_specs=(P(row, col), P(col, row), P(row, col)),
        out_specs=(P(col, row), P(row, col)),
        check_vma=False,
    )
```

```python
import functools

import jax
import jax.numpy as jnp
from jax import lax
from jax.experimental import pallas as pl
from jax.experimental.pallas import tpu as pltpu
from jax.sharding import Mesh
from jax.sharding import PartitionSpec as P

MXB = 32
CODE_LIMIT = 448.0
PEAK_FLOOR = 0.25
Y, ZH, ZL = 4, 8, 4
F32 = jnp.float32
BF16 = jnp.bfloat16


def block_scale(peaks):
    scale = jnp.full_like(peaks, 2.0 ** (-10))
    for power in range(-1, 8):
        scale = jnp.where(peaks >= 2.0**power, 2.0 ** (power - 8), scale)
    return scale


def requant(blocks, axis):
    peaks = jnp.maximum(jnp.max(jnp.abs(blocks), axis=axis, keepdims=True), PEAK_FLOOR)
    scale = block_scale(peaks)
    limit = CODE_LIMIT * scale
    held = jnp.minimum(jnp.maximum(blocks, -limit), limit) * (1.0 + 2.0**-12)
    wide = held * (2.0**20 + 1.0)
    normal = wide - (wide - held)
    anchor = (1.5 * 2.0**14) * scale
    small = (held + anchor) - anchor
    return jnp.where(jnp.abs(blocks) < 2.0**-6 * scale, small, normal)


def dot(a, b, dims):
    return lax.dot_general(a, b, (dims, ((), ())), preferred_element_type=F32)


def partial_kernel(at_ref, g_ref, w_ref, *out_refs):
    tok, ff = g_ref.shape
    g_t = g_ref[...].astype(F32).T
    codes_t = requant(g_t.reshape(ff // MXB, MXB, tok), 1).reshape(ff, tok).astype(BF16)
    chunk = tok // Y
    row = lax.broadcasted_iota(jnp.int32, (tok, tok), 0)
    col = lax.broadcasted_iota(jnp.int32, (tok, tok), 1)
    far, rest = row // chunk, row % chunk
    near, zh, pair = rest // (2 * ZH), rest % (2 * ZH) // 2, rest % 2
    source = (far + at_ref[0]) % Y * chunk + (zh * ZL + (near + at_ref[1]) % ZL) * 2 + pair
    order = jnp.where(col == source, 1.0, 0.0).astype(BF16)
    codes = dot(order, codes_t, ((1,), (1,))).astype(BF16)
    for d, out_ref in enumerate(out_refs):
        out_ref[...] = dot(codes[d * chunk : (d + 1) * chunk], w_ref[...], ((1,), (0,)))


def partial_sums(at, g, w_t):
    tok, ff = g.shape
    feat = w_t.shape[1]
    return pl.pallas_call(
        partial_kernel,
        out_shape=[jax.ShapeDtypeStruct((tok // Y, feat), F32)] * Y,
        in_specs=[
            pl.BlockSpec(memory_space=pltpu.SMEM),
            pl.BlockSpec(memory_space=pltpu.VMEM),
            pl.BlockSpec(memory_space=pltpu.VMEM),
        ],
        out_specs=[pl.BlockSpec(memory_space=pltpu.VMEM)] * Y,
        compiler_params=pltpu.CompilerParams(vmem_limit_bytes=32 * 2**20),
        cost_estimate=pl.CostEstimate(
            flops=2 * tok * ff * feat, bytes_accessed=2 * ff * feat + 4 * tok * feat, transcendentals=0
        ),
    )(at, g, w_t)


def weight_kernel(at_ref, g_ref, *refs):
    act_refs, out_ref, toks_ref, ahead_ref = refs[:Y], refs[Y], refs[Y + 1], refs[Y + 2]
    tok, ff = g_ref.shape
    chunk = tok // Y

    @pl.when(pl.program_id(0) == 0)
    def _():
        g = g_ref[...].astype(F32).reshape(tok // MXB, MXB, ff)
        ahead_ref[...] = requant(g, 1).reshape(tok, ff)
        parts = []
        for d in range(Y):
            start = pl.multiple_of((at_ref[0] + (Y - d)) % Y * chunk, chunk)
            parts.append(ahead_ref[pl.ds(start, chunk), :].T)
        toks_ref[...] = jnp.concatenate(parts, axis=1).astype(BF16)

    acts = []
    for act_ref in act_refs:
        a = act_ref[...].astype(F32)
        width = a.shape[1]
        acts.append(requant(a.reshape(chunk // MXB, MXB, width), 1).reshape(chunk, width).astype(BF16))
    out_ref[...] = dot(toks_ref[...], jnp.concatenate(acts, axis=0), ((1,), (0,))).astype(BF16)


def weight_grad(at, g, acts):
    tok, ff = g.shape
    feat = acts[0].shape[1]
    tile = feat // 4
    return pl.pallas_call(
        weight_kernel,
        out_shape=jax.ShapeDtypeStruct((ff, feat), BF16),
        grid=(feat // tile,),
        in_specs=[
            pl.BlockSpec(memory_space=pltpu.SMEM),
            pl.BlockSpec((tok, ff), lambda i: (0, 0)),
        ]
        + [pl.BlockSpec((tok // Y, tile), lambda i: (0, i))] * Y,
        out_specs=pl.BlockSpec((ff, tile), lambda i: (0, i)),
        scratch_shapes=[pltpu.VMEM((ff, tok), BF16), pltpu.VMEM((tok, ff), F32)],
        compiler_params=pltpu.CompilerParams(vmem_limit_bytes=32 * 2**20),
        cost_estimate=pl.CostEstimate(
            flops=2 * tok * ff * feat + 20 * tok * feat,
            bytes_accessed=2 * ff * feat + 2 * tok * feat,
            transcendentals=0,
        ),
    )(at, g, *acts)


def add_y_kernel(*refs):
    ins, outs = refs[:Y], refs[Y:]
    total = (ins[0][...] + ins[1][...]) + (ins[2][...] + ins[3][...])
    rows = total.shape[0] // ZL
    for e, out_ref in enumerate(outs):
        out_ref[...] = total[e * rows : (e + 1) * rows]


def add_y(parts):
    rows, feat = parts[0].shape
    return pl.pallas_call(
        add_y_kernel,
        out_shape=[jax.ShapeDtypeStruct((rows // ZL, feat), F32)] * ZL,
        compiler_params=pltpu.CompilerParams(vmem_limit_bytes=16 * 2**20),
        cost_estimate=pl.CostEstimate(flops=4 * rows * feat, bytes_accessed=20 * rows * feat, transcendentals=0),
    )(*parts)


def add_zl_kernel(*refs):
    ins, out_ref = refs[:ZL], refs[ZL]
    total = (ins[0][...] + ins[1][...]) + (ins[2][...] + ins[3][...])
    for h in range(ZH):
        out_ref[h] = total[2 * h : 2 * h + 2]


def add_zl(parts):
    rows, feat = parts[0].shape
    return pl.pallas_call(
        add_zl_kernel,
        out_shape=jax.ShapeDtypeStruct((ZH, rows // ZH, feat), F32),
        compiler_params=pltpu.CompilerParams(vmem_limit_bytes=16 * 2**20),
        cost_estimate=pl.CostEstimate(flops=4 * rows * feat, bytes_accessed=20 * rows * feat, transcendentals=0),
    )(*parts)


def along(x, axis, distance, size):
    return lax.ppermute(x, axis, [(k, (k + distance) % size) for k in range(size)])


def local(grad_out, acts, weight):
    at = jnp.stack([lax.axis_index("y"), lax.axis_index("zl")]).astype(jnp.int32)
    z = ZH * ZL
    rows, feat = acts.shape

    copies = jnp.broadcast_to(acts[None], (z, rows, feat))
    z_acts = lax.all_to_all(copies, ("zh", "zl"), 0, 0).reshape(z * rows, feat)
    g = lax.all_gather(grad_out, ("x", "core"), axis=0, tiled=True)

    sums = partial_sums(at, g, weight.T)
    pieces = add_y([sums[0]] + [along(sums[d], "y", d, Y) for d in (2, 1, 3)])
    total = add_zl([pieces[0]] + [along(pieces[e], "zl", e, ZL) for e in (1, 2, 3)])

    all_acts = [z_acts] + [along(z_acts, "y", d, Y) for d in (1, 2, 3)]

    parts = lax.all_to_all(total, "zh", 0, 0)
    grad_weight = weight_grad(at, g, all_acts).T
    grad_in = jnp.sum(parts, axis=0).astype(BF16)
    return grad_in, grad_weight


def solution(mesh):
    fine = Mesh(mesh.devices.reshape(4, 2, Y, ZH, ZL), ("x", "core", "y", "zh", "zl"))
    row, col = ("x", "core"), ("y", "zh", "zl")
    return jax.shard_map(
        local,
        mesh=fine,
        in_specs=(P(row, col), P(col, row), P(row, col)),
        out_specs=(P(col, row), P(row, col)),
        check_vma=False,
    )
```

```python
import jax
import jax.numpy as jnp
from jax import lax
from jax.experimental import pallas as pl
from jax.experimental.pallas import tpu as pltpu
from jax.sharding import Mesh
from jax.sharding import PartitionSpec as P

MXB = 32
CODE_LIMIT = 448.0
PEAK_FLOOR = 0.25
Y, ZH, ZL = 4, 8, 4
LANES = 128
SPAN = 125.0
F32 = jnp.float32
BF16 = jnp.bfloat16


def block_scale(peaks):
    scale = jnp.full_like(peaks, 2.0 ** (-10))
    for power in range(-1, 8):
        scale = jnp.where(peaks >= 2.0**power, 2.0 ** (power - 8), scale)
    return scale


def requant(blocks, axis):
    peaks = jnp.maximum(jnp.max(jnp.abs(blocks), axis=axis, keepdims=True), PEAK_FLOOR)
    scale = block_scale(peaks)
    limit = CODE_LIMIT * scale
    held = jnp.minimum(jnp.maximum(blocks, -limit), limit) * (1.0 + 2.0**-12)
    wide = held * (2.0**20 + 1.0)
    normal = wide - (wide - held)
    anchor = (1.5 * 2.0**14) * scale
    small = (held + anchor) - anchor
    return jnp.where(jnp.abs(blocks) < 2.0**-6 * scale, small, normal)


def dot(a, b, dims):
    return lax.dot_general(a, b, (dims, ((), ())), preferred_element_type=F32)


def encode(values):
    top = jnp.max(jnp.abs(values), axis=1, keepdims=True)
    top = (jnp.maximum(top, 2.0**-90) * (1.0 + 2.0**-7)).astype(BF16)
    step = (2.0 * SPAN) / top.astype(F32)
    level = jnp.exp2(jnp.abs(values) * step - SPAN)
    codes = jnp.where(values < 0.0, -level, level).astype(BF16)
    return codes, jnp.broadcast_to(top, (values.shape[0], LANES))


def decode(codes, top):
    code = codes.astype(F32)
    step = top[:, :1].astype(F32) * (1.0 / (2.0 * SPAN))
    magnitude = (jnp.log2(jnp.abs(code)) + SPAN) * step
    return jnp.where(code < 0.0, -magnitude, magnitude)


def decoded_sum(in_refs):
    feat = in_refs[0].shape[1] - LANES
    parts = [decode(in_ref[:, :feat], in_ref[:, feat:]) for in_ref in in_refs]
    return (parts[0] + parts[1]) + (parts[2] + parts[3])


def partial_kernel(at_ref, g_ref, w_hbm, *refs):
    out_refs, w_ref, sem = refs[:Y], refs[Y], refs[Y + 1]
    copy = pltpu.make_async_copy(w_hbm, w_ref, sem)
    copy.start()
    tok, ff = g_ref.shape
    feat = w_ref.shape[1]
    g_t = g_ref[...].astype(F32).T
    codes_t = requant(g_t.reshape(ff // MXB, MXB, tok), 1).reshape(ff, tok).astype(BF16)
    chunk = tok // Y
    row = lax.broadcasted_iota(jnp.int32, (tok, tok), 0)
    col = lax.broadcasted_iota(jnp.int32, (tok, tok), 1)
    far, rest = row // chunk, row % chunk
    near, zh, pair = rest // (2 * ZH), rest % (2 * ZH) // 2, rest % 2
    source = (far + at_ref[0]) % Y * chunk + (zh * ZL + (near + at_ref[1]) % ZL) * 2 + pair
    order = jnp.where(col == source, 1.0, 0.0).astype(BF16)
    held = dot(order, codes_t, ((1,), (1,))).astype(BF16)
    copy.wait()
    for d, out_ref in enumerate(out_refs):
        codes, top = encode(dot(held[d * chunk : (d + 1) * chunk], w_ref[...], ((1,), (0,))))
        out_ref[:, :feat] = codes
        out_ref[:, feat:] = top


def partial_sums(at, g, w_t):
    tok, ff = g.shape
    feat = w_t.shape[1]
    return pl.pallas_call(
        partial_kernel,
        out_shape=[jax.ShapeDtypeStruct((tok // Y, feat + LANES), BF16)] * Y,
        in_specs=[
            pl.BlockSpec(memory_space=pltpu.SMEM),
            pl.BlockSpec(memory_space=pltpu.VMEM),
            pl.BlockSpec(memory_space=pltpu.HBM),
        ],
        out_specs=[pl.BlockSpec(memory_space=pltpu.VMEM)] * Y,
        scratch_shapes=[pltpu.VMEM((ff, feat), BF16), pltpu.SemaphoreType.DMA],
        compiler_params=pltpu.CompilerParams(vmem_limit_bytes=58 * 2**20),
        cost_estimate=pl.CostEstimate(
            flops=2 * tok * ff * feat, bytes_accessed=2 * ff * feat + 2 * tok * feat, transcendentals=tok * feat
        ),
    )(at, g, w_t)


def add_y_kernel(*refs):
    feat = refs[0].shape[1] - LANES
    rows = refs[Y].shape[0]
    codes, top = encode(decoded_sum(refs[:Y]))
    for e, out_ref in enumerate(refs[Y:]):
        out_ref[:, :feat] = codes[e * rows : (e + 1) * rows]
        out_ref[:, feat:] = top[e * rows : (e + 1) * rows]


def add_zl_kernel(*refs):
    total = decoded_sum(refs[:ZL])
    for k in range(ZH):
        refs[ZL][k] = total[2 * k : 2 * k + 2]


def add_call(kernel, parts, out_shape):
    size = len(parts) * parts[0].size
    return pl.pallas_call(
        kernel,
        out_shape=out_shape,
        compiler_params=pltpu.CompilerParams(vmem_limit_bytes=16 * 2**20),
        cost_estimate=pl.CostEstimate(flops=10 * size, bytes_accessed=4 * size, transcendentals=size),
    )(*parts)


def weight_kernel(at_ref, g_ref, *refs):
    act_refs, (out_ref, done_ref, toks_ref, ahead_ref) = refs[:Y], refs[Y:]
    tok, ff = g_ref.shape
    chunk = tok // Y

    @pl.when(pl.program_id(0) == 0)
    def _():
        g = g_ref[...].astype(F32).reshape(tok // MXB, MXB, ff)
        ahead_ref[...] = requant(g, 1).reshape(tok, ff)
        parts = []
        for d in range(Y):
            start = pl.multiple_of((at_ref[0] + (Y - d)) % Y * chunk, chunk)
            parts.append(ahead_ref[pl.ds(start, chunk), :].T)
        toks_ref[...] = jnp.concatenate(parts, axis=1).astype(BF16)
        done_ref[...] = jnp.zeros_like(done_ref)

    acts = []
    for act_ref in act_refs:
        a = act_ref[...].astype(F32)
        width = a.shape[1]
        acts.append(requant(a.reshape(chunk // MXB, MXB, width), 1).reshape(chunk, width).astype(BF16))
    out_ref[...] = dot(toks_ref[...], jnp.concatenate(acts, axis=0), ((1,), (0,))).astype(BF16)


def weight_grad(at, g, acts):
    tok, ff = g.shape
    feat = acts[0].shape[1]
    tile = feat // 4
    return pl.pallas_call(
        weight_kernel,
        out_shape=[jax.ShapeDtypeStruct((ff, feat), BF16), jax.ShapeDtypeStruct((8, LANES), F32)],
        grid=(feat // tile,),
        in_specs=[
            pl.BlockSpec(memory_space=pltpu.SMEM),
            pl.BlockSpec((tok, ff), lambda i: (0, 0)),
        ]
        + [pl.BlockSpec((tok // Y, tile), lambda i: (0, i))] * Y,
        out_specs=[pl.BlockSpec((ff, tile), lambda i: (0, i)), pl.BlockSpec((8, LANES), lambda i: (0, 0))],
        scratch_shapes=[pltpu.VMEM((ff, tok), BF16), pltpu.VMEM((tok, ff), F32)],
        compiler_params=pltpu.CompilerParams(vmem_limit_bytes=32 * 2**20),
        cost_estimate=pl.CostEstimate(
            flops=2 * tok * ff * feat + 20 * tok * feat,
            bytes_accessed=2 * ff * feat + 2 * tok * feat,
            transcendentals=0,
        ),
    )(at, g, *acts)


def add_zh_kernel(in_ref, done_ref, out_ref):
    total = in_ref[0]
    for k in range(1, ZH):
        total = total + in_ref[k]
    out_ref[...] = total.astype(BF16)


def add_zh(parts, done):
    return pl.pallas_call(
        add_zh_kernel,
        out_shape=jax.ShapeDtypeStruct(parts.shape[1:], BF16),
        compiler_params=pltpu.CompilerParams(vmem_limit_bytes=16 * 2**20),
        cost_estimate=pl.CostEstimate(flops=parts.size, bytes_accessed=4 * parts.size, transcendentals=0),
    )(parts, done)


def along(x, axis, distance, size):
    return lax.ppermute(x, axis, [(k, (k + distance) % size) for k in range(size)])


def local(grad_out, acts, weight):
    at = jnp.stack([lax.axis_index("y"), lax.axis_index("zl")]).astype(jnp.int32)
    rows, feat = acts.shape
    z = ZH * ZL

    copies = jnp.broadcast_to(acts[None], (z, rows, feat))
    z_acts = lax.all_to_all(copies, ("zh", "zl"), 0, 0).reshape(z * rows, feat)
    g = lax.all_gather(grad_out, ("x", "core"), axis=0, tiled=True)

    sums = partial_sums(at, g, weight.T)
    sums = [sums[0]] + [along(sums[d], "y", d, Y) for d in (2, 1, 3)]
    sums = add_call(add_y_kernel, sums, [jax.ShapeDtypeStruct((ZH * rows, feat + LANES), BF16)] * ZL)
    sums = [sums[0]] + [along(sums[e], "zl", e, ZL) for e in (1, 2, 3)]
    sums = add_call(add_zl_kernel, sums, jax.ShapeDtypeStruct((ZH, rows, feat), F32))

    all_acts = [z_acts] + [along(z_acts, "y", d, Y) for d in (1, 2, 3)]
    sums = lax.all_to_all(sums, "zh", 0, 0)
    grad_weight_t, done = weight_grad(at, g, all_acts)
    return add_zh(sums, done), grad_weight_t.T


def solution(mesh):
    fine = Mesh(mesh.devices.reshape(4, 2, Y, ZH, ZL), ("x", "core", "y", "zh", "zl"))
    row, col = ("x", "core"), ("y", "zh", "zl")
    return jax.shard_map(
        local,
        mesh=fine,
        in_specs=(P(row, col), P(col, row), P(row, col)),
        out_specs=(P(col, row), P(row, col)),
        check_vma=False,
    )
```

```python
import jax
import jax.numpy as jnp
from jax import lax
from jax.experimental import pallas as pl
from jax.experimental.pallas import tpu as pltpu
from jax.sharding import Mesh
from jax.sharding import PartitionSpec as P

MXB = 32
CODE_LIMIT = 448.0
PEAK_FLOOR = 0.25
Y, ZH, ZM, Z0 = 4, 8, 2, 2
ZL = ZM * Z0
Z16 = ZH * ZM
LANES = 128
SPAN = 125.0
F32 = jnp.float32
BF16 = jnp.bfloat16


def block_scale(peaks):
    scale = jnp.full_like(peaks, 2.0 ** (-10))
    for power in range(-1, 8):
        scale = jnp.where(peaks >= 2.0**power, 2.0 ** (power - 8), scale)
    return scale


def requant(blocks, axis):
    peaks = jnp.maximum(jnp.max(jnp.abs(blocks), axis=axis, keepdims=True), PEAK_FLOOR)
    scale = block_scale(peaks)
    limit = CODE_LIMIT * scale
    held = jnp.minimum(jnp.maximum(blocks, -limit), limit) * (1.0 + 2.0**-12)
    wide = held * (2.0**20 + 1.0)
    normal = wide - (wide - held)
    anchor = (1.5 * 2.0**14) * scale
    small = (held + anchor) - anchor
    return jnp.where(jnp.abs(blocks) < 2.0**-6 * scale, small, normal)


def dot(a, b, dims):
    return lax.dot_general(a, b, (dims, ((), ())), preferred_element_type=F32)


def encode(values):
    top = jnp.max(jnp.abs(values), axis=1, keepdims=True)
    top = (jnp.maximum(top, 2.0**-90) * (1.0 + 2.0**-7)).astype(BF16)
    step = (2.0 * SPAN) / top.astype(F32)
    level = jnp.exp2(jnp.abs(values) * step - SPAN)
    codes = jnp.where(values < 0.0, -level, level).astype(BF16)
    return codes, jnp.broadcast_to(top, (values.shape[0], LANES))


def decode(codes, top):
    code = codes.astype(F32)
    step = top[:, :1].astype(F32) * (1.0 / (2.0 * SPAN))
    magnitude = (jnp.log2(jnp.abs(code)) + SPAN) * step
    return jnp.where(code < 0.0, -magnitude, magnitude)


def decoded_sum(in_ref):
    feat = in_ref.shape[2] - LANES
    total = decode(in_ref[0, :, :feat], in_ref[0, :, feat:])
    for k in range(1, in_ref.shape[0]):
        total = total + decode(in_ref[k, :, :feat], in_ref[k, :, feat:])
    return total


def partial_kernel(g_ref, w_hbm, out_ref, w_ref, sem):
    copy = pltpu.make_async_copy(w_hbm, w_ref, sem)
    copy.start()
    tok, ff = g_ref.shape
    feat = w_ref.shape[1]
    g_t = g_ref[...].astype(F32).T
    codes_t = requant(g_t.reshape(ff // MXB, MXB, tok), 1).reshape(ff, tok).astype(BF16)
    row = lax.broadcasted_iota(jnp.int32, (tok, tok), 0)
    col = lax.broadcasted_iota(jnp.int32, (tok, tok), 1)
    rows = tok // (Y * Z0)
    place, rest = row // rows, row % rows
    source = place // Z0 * (rows * Z0) + (rest // 2 * Z0 + place % Z0) * 2 + rest % 2
    order = jnp.where(col == source, 1.0, 0.0).astype(BF16)
    held = dot(order, codes_t, ((1,), (1,))).astype(BF16)
    copy.wait()
    for k in range(Y * Z0):
        codes, top = encode(dot(held[k * rows : (k + 1) * rows], w_ref[...], ((1,), (0,))))
        out_ref[k, :, :feat] = codes
        out_ref[k, :, feat:] = top


def partial_sums(g, w_t):
    tok, ff = g.shape
    feat = w_t.shape[1]
    return pl.pallas_call(
        partial_kernel,
        out_shape=jax.ShapeDtypeStruct((Y * Z0, tok // (Y * Z0), feat + LANES), BF16),
        in_specs=[pl.BlockSpec(memory_space=pltpu.VMEM), pl.BlockSpec(memory_space=pltpu.HBM)],
        out_specs=pl.BlockSpec(memory_space=pltpu.VMEM),
        scratch_shapes=[pltpu.VMEM((ff, feat), BF16), pltpu.SemaphoreType.DMA],
        compiler_params=pltpu.CompilerParams(vmem_limit_bytes=58 * 2**20),
        cost_estimate=pl.CostEstimate(
            flops=2 * tok * ff * feat, bytes_accessed=2 * ff * feat + 2 * tok * feat, transcendentals=tok * feat
        ),
    )(g, w_t)


def add_near_kernel(in_ref, *refs):
    act_refs, (out_ref, acts_ref) = refs[:ZL], refs[ZL:]
    feat = in_ref.shape[2] - LANES
    codes, top = encode(decoded_sum(in_ref))
    for k in range(Z16):
        out_ref[k, :, :feat] = codes[2 * k : 2 * k + 2]
        out_ref[k, :, feat:] = top[2 * k : 2 * k + 2]
    acts_ref[...] = jnp.concatenate([act_ref[...] for act_ref in act_refs], axis=0)


def add_near(parts, acts):
    places, rows, wide = parts.shape
    return pl.pallas_call(
        add_near_kernel,
        out_shape=[
            jax.ShapeDtypeStruct((Z16, rows // Z16, wide), BF16),
            jax.ShapeDtypeStruct((ZL * acts[0].shape[0], acts[0].shape[1]), BF16),
        ],
        compiler_params=pltpu.CompilerParams(vmem_limit_bytes=16 * 2**20),
        cost_estimate=pl.CostEstimate(flops=10 * parts.size, bytes_accessed=2 * parts.size, transcendentals=parts.size),
    )(parts, *acts)


def add_far_kernel(in_ref, done_ref, out_ref):
    out_ref[...] = decoded_sum(in_ref).astype(BF16)


def add_far(parts, done):
    places, rows, wide = parts.shape
    return pl.pallas_call(
        add_far_kernel,
        out_shape=jax.ShapeDtypeStruct((rows, wide - LANES), BF16),
        compiler_params=pltpu.CompilerParams(vmem_limit_bytes=16 * 2**20),
        cost_estimate=pl.CostEstimate(flops=10 * parts.size, bytes_accessed=2 * parts.size, transcendentals=parts.size),
    )(parts, done)


def weight_kernel(at_ref, g_ref, *refs):
    act_refs, (out_ref, done_ref, toks_ref) = refs[:Y], refs[Y:]
    tok, ff = g_ref.shape
    chunk = tok // Y

    @pl.when(pl.program_id(0) == 0)
    def _():
        g = requant(g_ref[...].astype(F32).reshape(tok // MXB, MXB, ff), 1).reshape(tok, ff).astype(BF16)
        row = lax.broadcasted_iota(jnp.int32, (tok, tok), 0)
        col = lax.broadcasted_iota(jnp.int32, (tok, tok), 1)
        far, rest = col // chunk, col % chunk
        near, zh, pair = rest // (2 * ZH), rest % (2 * ZH) // 2, rest % 2
        y, zl = (at_ref[0] + Y - far) % Y, (at_ref[1] + ZL - near) % ZL
        order = jnp.where(row == y * chunk + (zh * ZL + zl) * 2 + pair, 1.0, 0.0).astype(BF16)
        toks_ref[...] = dot(g, order, ((0,), (0,))).astype(BF16)
        done_ref[...] = jnp.zeros_like(done_ref)

    acts = []
    for act_ref in act_refs:
        a = act_ref[...].astype(F32)
        width = a.shape[1]
        blocks = a.reshape(ZL, 2 * ZH // 8, 8, width)
        for_blocks = [requant(blocks[:, b].reshape(MXB, width), 0).reshape(ZL, 8, width) for b in range(2 * ZH // 8)]
        acts.append(jnp.stack(for_blocks, axis=1).reshape(chunk, width).astype(BF16))
    out_ref[...] = dot(toks_ref[...], jnp.concatenate(acts, axis=0), ((1,), (0,))).astype(BF16)


def weight_grad(at, g, acts):
    tok, ff = g.shape
    feat = acts[0].shape[1]
    tile = feat // 4
    return pl.pallas_call(
        weight_kernel,
        out_shape=[jax.ShapeDtypeStruct((ff, feat), BF16), jax.ShapeDtypeStruct((8, LANES), F32)],
        grid=(feat // tile,),
        in_specs=[
            pl.BlockSpec(memory_space=pltpu.SMEM),
            pl.BlockSpec((tok, ff), lambda i: (0, 0)),
        ]
        + [pl.BlockSpec((tok // Y, tile), lambda i: (0, i))] * Y,
        out_specs=[pl.BlockSpec((ff, tile), lambda i: (0, i)), pl.BlockSpec((8, LANES), lambda i: (0, 0))],
        scratch_shapes=[pltpu.VMEM((ff, tok), BF16)],
        compiler_params=pltpu.CompilerParams(vmem_limit_bytes=32 * 2**20),
        cost_estimate=pl.CostEstimate(
            flops=2 * tok * ff * feat + 20 * tok * feat,
            bytes_accessed=2 * ff * feat + 2 * tok * feat,
            transcendentals=0,
        ),
    )(at, g, *acts)


def along(x, axis, distance, size):
    return lax.ppermute(x, axis, [(k, (k + distance) % size) for k in range(size)])


def local(grad_out, acts, weight):
    rows, feat = acts.shape
    near = lax.axis_index("zm") * Z0 + lax.axis_index("z0")
    at = jnp.stack([lax.axis_index("y"), near]).astype(jnp.int32)

    copies = jnp.broadcast_to(acts[None], (ZH, rows, feat))
    zh_acts = lax.all_to_all(copies, "zh", 0, 0).reshape(ZH * rows, feat)
    g = lax.all_gather(grad_out, ("x", "core"), axis=0, tiled=True)

    sums = lax.all_to_all(partial_sums(g, weight.T), ("y", "z0"), 0, 0)
    near_acts = [zh_acts] + [along(zh_acts, ("zm", "z0"), e, ZL) for e in (1, 2, 3)]
    sums, z_acts = add_near(sums, near_acts)
    sums = lax.all_to_all(sums, ("zh", "zm"), 0, 0)
    all_acts = [z_acts] + [along(z_acts, "y", d, Y) for d in (1, 2, 3)]
    grad_weight_t, done = weight_grad(at, g, all_acts)
    return add_far(sums, done), grad_weight_t.T


def solution(mesh):
    fine = Mesh(mesh.devices.reshape(4, 2, Y, ZH, ZM, Z0), ("x", "core", "y", "zh", "zm", "z0"))
    row, col = ("x", "core"), ("y", "zh", "zm", "z0")
    return jax.shard_map(
        local,
        mesh=fine,
        in_specs=(P(row, col), P(col, row), P(row, col)),
        out_specs=(P(col, row), P(row, col)),
        check_vma=False,
    )
```

```python
import jax
import jax.numpy as jnp
from jax import lax
from jax.experimental import pallas as pl
from jax.experimental.pallas import tpu as pltpu
from jax.sharding import Mesh
from jax.sharding import PartitionSpec as P

MXB = 32
CODE_LIMIT = 448.0
PEAK_FLOOR = 0.25
Y, ZH, ZM, Z0 = 4, 8, 2, 2
ZL = ZM * Z0
Z16 = ZH * ZM
LANES = 128
TILES = 4
SPAN = 125.0
F32 = jnp.float32
BF16 = jnp.bfloat16


def block_scale(peaks):
    scale = jnp.full_like(peaks, 2.0 ** (-10))
    for power in range(-1, 8):
        scale = jnp.where(peaks >= 2.0**power, 2.0 ** (power - 8), scale)
    return scale


def requant(blocks, axis):
    peaks = jnp.maximum(jnp.max(jnp.abs(blocks), axis=axis, keepdims=True), PEAK_FLOOR)
    scale = block_scale(peaks)
    limit = CODE_LIMIT * scale
    held = jnp.minimum(jnp.maximum(blocks, -limit), limit) * (1.0 + 2.0**-12)
    wide = held * (2.0**20 + 1.0)
    normal = wide - (wide - held)
    anchor = (1.5 * 2.0**14) * scale
    small = (held + anchor) - anchor
    return jnp.where(jnp.abs(blocks) < 2.0**-6 * scale, small, normal)


def dot(a, b, dims):
    return lax.dot_general(a, b, (dims, ((), ())), preferred_element_type=F32)


def top_of(magnitude):
    return (jnp.maximum(magnitude, 2.0**-90) * (1.0 + 2.0**-7)).astype(BF16)


def encode_with(values, top):
    level = jnp.exp2(jnp.abs(values) * ((2.0 * SPAN) / top.astype(F32)) - SPAN)
    return jnp.where(values < 0.0, -level, level).astype(BF16)


def encode(values):
    top = top_of(jnp.max(jnp.abs(values), axis=1, keepdims=True))
    return encode_with(values, top), jnp.broadcast_to(top, (values.shape[0], LANES))


def decode(codes, top):
    code = codes.astype(F32)
    step = top[:, :1].astype(F32) * (1.0 / (2.0 * SPAN))
    magnitude = (jnp.log2(jnp.abs(code)) + SPAN) * step
    return jnp.where(code < 0.0, -magnitude, magnitude)


def decoded_sum(in_ref):
    feat = in_ref.shape[2] - LANES
    total = decode(in_ref[0, :, :feat], in_ref[0, :, feat:])
    for k in range(1, in_ref.shape[0]):
        total = total + decode(in_ref[k, :, :feat], in_ref[k, :, feat:])
    return total


def partial_kernel(g_ref, w_hbm, out_ref, w_ref, sums_ref, sems):
    tok, ff = g_ref.shape
    feat = w_ref.shape[1]
    tile = feat // TILES
    tiles = [slice(t * tile, (t + 1) * tile) for t in range(TILES)]
    copies = [pltpu.make_async_copy(w_hbm.at[:, c], w_ref.at[:, c], sems.at[t]) for t, c in enumerate(tiles)]
    for copy in copies:
        copy.start()
    g_t = g_ref[...].astype(F32).T
    codes_t = requant(g_t.reshape(ff // MXB, MXB, tok), 1).reshape(ff, tok).astype(BF16)
    row = lax.broadcasted_iota(jnp.int32, (tok, tok), 0)
    col = lax.broadcasted_iota(jnp.int32, (tok, tok), 1)
    rows = tok // (Y * Z0)
    place, rest = row // rows, row % rows
    source = place // Z0 * (rows * Z0) + (rest // 2 * Z0 + place % Z0) * 2 + rest % 2
    order = jnp.where(col == source, 1.0, 0.0).astype(BF16)
    held = dot(order, codes_t, ((1,), (1,))).astype(BF16)
    most = jnp.zeros((tok, LANES), F32)
    for copy, c in zip(copies, tiles):
        copy.wait()
        part = dot(held, w_ref[:, c], ((1,), (0,)))
        sums_ref[:, c] = part
        for k in range(tile // LANES):
            most = jnp.maximum(most, jnp.abs(part[:, k * LANES : (k + 1) * LANES]))
    top = top_of(jnp.max(most, axis=1, keepdims=True))
    wide = jnp.broadcast_to(top, (tok, LANES))
    for k in range(Y * Z0):
        r = slice(k * rows, (k + 1) * rows)
        out_ref[k, :, :feat] = encode_with(sums_ref[r, :], top[r])
        out_ref[k, :, feat:] = wide[r]


def partial_sums(g, w_t):
    tok, ff = g.shape
    feat = w_t.shape[1]
    return pl.pallas_call(
        partial_kernel,
        out_shape=jax.ShapeDtypeStruct((Y * Z0, tok // (Y * Z0), feat + LANES), BF16),
        in_specs=[pl.BlockSpec(memory_space=pltpu.VMEM), pl.BlockSpec(memory_space=pltpu.HBM)],
        out_specs=pl.BlockSpec(memory_space=pltpu.VMEM),
        scratch_shapes=[
            pltpu.VMEM((ff, feat), BF16),
            pltpu.VMEM((tok, feat), F32),
            pltpu.SemaphoreType.DMA((TILES,)),
        ],
        compiler_params=pltpu.CompilerParams(vmem_limit_bytes=58 * 2**20),
        cost_estimate=pl.CostEstimate(
            flops=2 * tok * ff * feat, bytes_accessed=2 * ff * feat + 2 * tok * feat, transcendentals=tok * feat
        ),
    )(g, w_t)


def add_near_kernel(in_ref, acts_ref, out_ref):
    feat = in_ref.shape[2] - LANES
    codes, top = encode(decoded_sum(in_ref))
    for k in range(Z16):
        out_ref[k, :, :feat] = codes[2 * k : 2 * k + 2]
        out_ref[k, :, feat:] = top[2 * k : 2 * k + 2]


def add_near(parts, acts):
    places, rows, wide = parts.shape
    return pl.pallas_call(
        add_near_kernel,
        out_shape=jax.ShapeDtypeStruct((Z16, rows // Z16, wide), BF16),
        grid=(1,),
        in_specs=[
            pl.BlockSpec(parts.shape, lambda i: (0, 0, 0)),
            pl.BlockSpec((16, LANES), lambda i: (0, 0)),
        ],
        out_specs=pl.BlockSpec((Z16, rows // Z16, wide), lambda i: (0, 0, 0)),
        compiler_params=pltpu.CompilerParams(vmem_limit_bytes=16 * 2**20),
        cost_estimate=pl.CostEstimate(flops=10 * parts.size, bytes_accessed=2 * parts.size, transcendentals=parts.size),
    )(parts, acts)


def add_far_kernel(in_ref, done_ref, out_ref):
    out_ref[...] = decoded_sum(in_ref).astype(BF16)


def add_far(parts, done):
    places, rows, wide = parts.shape
    return pl.pallas_call(
        add_far_kernel,
        out_shape=jax.ShapeDtypeStruct((rows, wide - LANES), BF16),
        compiler_params=pltpu.CompilerParams(vmem_limit_bytes=16 * 2**20),
        cost_estimate=pl.CostEstimate(flops=10 * parts.size, bytes_accessed=2 * parts.size, transcendentals=parts.size),
    )(parts, done)


def weight_kernel(at_ref, g_ref, *refs):
    act_refs, (out_ref, done_ref, toks_ref) = refs[:Y], refs[Y:]
    tok, ff = g_ref.shape
    chunk = tok // Y

    @pl.when(pl.program_id(0) == 0)
    def _():
        g = requant(g_ref[...].astype(F32).reshape(tok // MXB, MXB, ff), 1).reshape(tok, ff).astype(BF16)
        row = lax.broadcasted_iota(jnp.int32, (tok, tok), 0)
        col = lax.broadcasted_iota(jnp.int32, (tok, tok), 1)
        far, rest = col // chunk, col % chunk
        near, zh, pair = rest // (2 * ZH), rest % (2 * ZH) // 2, rest % 2
        y = (at_ref[0] + Y - far) % Y
        order = jnp.where(row == y * chunk + (zh * ZL + near) * 2 + pair, 1.0, 0.0).astype(BF16)
        toks_ref[...] = dot(g, order, ((0,), (0,))).astype(BF16)
        done_ref[...] = jnp.zeros_like(done_ref)

    acts = []
    for act_ref in act_refs:
        a = act_ref[...].astype(F32)
        width = a.shape[1]
        blocks = a.reshape(ZL, 2 * ZH // 8, 8, width)
        for_blocks = [requant(blocks[:, b].reshape(MXB, width), 0).reshape(ZL, 8, width) for b in range(2 * ZH // 8)]
        acts.append(jnp.stack(for_blocks, axis=1).reshape(chunk, width).astype(BF16))
    out_ref[...] = dot(toks_ref[...], jnp.concatenate(acts, axis=0), ((1,), (0,))).astype(BF16)


def weight_grad(at, g, acts):
    tok, ff = g.shape
    feat = acts[0].shape[1]
    tile = feat // 4
    return pl.pallas_call(
        weight_kernel,
        out_shape=[jax.ShapeDtypeStruct((ff, feat), BF16), jax.ShapeDtypeStruct((8, LANES), F32)],
        grid=(feat // tile,),
        in_specs=[
            pl.BlockSpec(memory_space=pltpu.SMEM),
            pl.BlockSpec((tok, ff), lambda i: (0, 0)),
        ]
        + [pl.BlockSpec((tok // Y, tile), lambda i: (0, i))] * Y,
        out_specs=[pl.BlockSpec((ff, tile), lambda i: (0, i)), pl.BlockSpec((8, LANES), lambda i: (0, 0))],
        scratch_shapes=[pltpu.VMEM((ff, tok), BF16)],
        compiler_params=pltpu.CompilerParams(vmem_limit_bytes=32 * 2**20),
        cost_estimate=pl.CostEstimate(
            flops=2 * tok * ff * feat + 20 * tok * feat,
            bytes_accessed=2 * ff * feat + 2 * tok * feat,
            transcendentals=0,
        ),
    )(at, g, *acts)


def along(x, axis, distance, size):
    return lax.ppermute(x, axis, [(k, (k + distance) % size) for k in range(size)])


def local(grad_out, acts, weight):
    rows, feat = acts.shape
    at = lax.axis_index("y").astype(jnp.int32).reshape(1)

    copies = jnp.broadcast_to(acts[None], (ZH, rows, feat))
    zh_acts = lax.all_to_all(copies, "zh", 0, 0).reshape(ZH * rows, feat)
    g = lax.all_gather(grad_out, ("x", "core"), axis=0, tiled=True)

    sums = lax.all_to_all(partial_sums(g, weight.T), ("y", "z0"), 0, 0)
    z_acts = lax.all_gather(zh_acts, ("zm", "z0"), axis=0, tiled=True)
    sums = lax.all_to_all(add_near(sums, z_acts), ("zh", "zm"), 0, 0)
    all_acts = [z_acts] + [along(z_acts, "y", d, Y) for d in (1, 2, 3)]
    grad_weight_t, done = weight_grad(at, g, all_acts)
    return add_far(sums, done), grad_weight_t.T


def solution(mesh):
    fine = Mesh(mesh.devices.reshape(4, 2, Y, ZH, ZM, Z0), ("x", "core", "y", "zh", "zm", "z0"))
    row, col = ("x", "core"), ("y", "zh", "zm", "z0")
    return jax.shard_map(
        local,
        mesh=fine,
        in_specs=(P(row, col), P(col, row), P(row, col)),
        out_specs=(P(col, row), P(row, col)),
        check_vma=False,
    )
```

```python
import jax
import jax.numpy as jnp
from jax import lax
from jax.experimental import pallas as pl
from jax.experimental.pallas import tpu as pltpu
from jax.sharding import Mesh
from jax.sharding import PartitionSpec as P

MXB = 32
CODE_LIMIT = 448.0
PEAK_FLOOR = 0.25
Y, ZH, ZM, Z0 = 4, 8, 2, 2
ZL = ZM * Z0
Z16 = ZH * ZM
LANES = 128
TILES = 4
SPAN = 125.0
F32 = jnp.float32
BF16 = jnp.bfloat16


def block_scale(peaks):
    scale = jnp.full_like(peaks, 2.0 ** (-10))
    for power in range(-1, 8):
        scale = jnp.where(peaks >= 2.0**power, 2.0 ** (power - 8), scale)
    return scale


def requant(blocks, axis):
    peaks = jnp.maximum(jnp.max(jnp.abs(blocks), axis=axis, keepdims=True), PEAK_FLOOR)
    scale = block_scale(peaks)
    limit = CODE_LIMIT * scale
    held = jnp.minimum(jnp.maximum(blocks, -limit), limit) * (1.0 + 2.0**-12)
    wide = held * (2.0**20 + 1.0)
    normal = wide - (wide - held)
    anchor = (1.5 * 2.0**14) * scale
    small = (held + anchor) - anchor
    return jnp.where(jnp.abs(blocks) < 2.0**-6 * scale, small, normal)


def dot(a, b, dims):
    return lax.dot_general(a, b, (dims, ((), ())), preferred_element_type=F32)


def top_of(magnitude):
    return (jnp.maximum(magnitude, 2.0**-90) * (1.0 + 2.0**-7)).astype(BF16)


def encode_with(values, top):
    level = jnp.exp2(jnp.abs(values) * ((2.0 * SPAN) / top.astype(F32)) - SPAN)
    return jnp.where(values < 0.0, -level, level).astype(BF16)


def encode(values):
    top = top_of(jnp.max(jnp.abs(values), axis=1, keepdims=True))
    return encode_with(values, top), jnp.broadcast_to(top, (values.shape[0], LANES))


def decode(codes, top):
    code = codes.astype(F32)
    step = top[:, :1].astype(F32) * (1.0 / (2.0 * SPAN))
    magnitude = (jnp.log2(jnp.abs(code)) + SPAN) * step
    return jnp.where(code < 0.0, -magnitude, magnitude)


def decoded_sum(in_ref):
    feat = in_ref.shape[2] - LANES
    total = decode(in_ref[0, :, :feat], in_ref[0, :, feat:])
    for k in range(1, in_ref.shape[0]):
        total = total + decode(in_ref[k, :, :feat], in_ref[k, :, feat:])
    return total


def partial_kernel(g_ref, w_hbm, out_ref, w_ref, sums_ref, sems):
    tok, ff = g_ref.shape
    feat = w_ref.shape[1]
    tile = feat // TILES
    tiles = [slice(t * tile, (t + 1) * tile) for t in range(TILES)]
    copies = [pltpu.make_async_copy(w_hbm.at[:, c], w_ref.at[:, c], sems.at[t]) for t, c in enumerate(tiles)]
    for copy in copies:
        copy.start()
    g_t = g_ref[...].astype(F32).T
    codes_t = requant(g_t.reshape(ff // MXB, MXB, tok), 1).reshape(ff, tok).astype(BF16)
    rows = tok // (Y * Z0)
    held = dot(ordered((tok, tok), 0), codes_t, ((1,), (1,))).astype(BF16)
    most = jnp.zeros((tok, LANES), F32)
    for copy, c in zip(copies, tiles):
        copy.wait()
        part = dot(held, w_ref[:, c], ((1,), (0,)))
        sums_ref[:, c] = part
        for k in range(tile // LANES):
            most = jnp.maximum(most, jnp.abs(part[:, k * LANES : (k + 1) * LANES]))
    top = top_of(jnp.max(most, axis=1, keepdims=True))
    wide = jnp.broadcast_to(top, (tok, LANES))
    for k in range(Y * Z0):
        r = slice(k * rows, (k + 1) * rows)
        out_ref[k, :, :feat] = encode_with(sums_ref[r, :], top[r])
        out_ref[k, :, feat:] = wide[r]


def partial_sums(g, w_t):
    tok, ff = g.shape
    feat = w_t.shape[1]
    return pl.pallas_call(
        partial_kernel,
        out_shape=jax.ShapeDtypeStruct((Y * Z0, tok // (Y * Z0), feat + LANES), BF16),
        in_specs=[pl.BlockSpec(memory_space=pltpu.VMEM), pl.BlockSpec(memory_space=pltpu.HBM)],
        out_specs=pl.BlockSpec(memory_space=pltpu.VMEM),
        scratch_shapes=[
            pltpu.VMEM((ff, feat), BF16),
            pltpu.VMEM((tok, feat), F32),
            pltpu.SemaphoreType.DMA((TILES,)),
        ],
        compiler_params=pltpu.CompilerParams(vmem_limit_bytes=58 * 2**20),
        cost_estimate=pl.CostEstimate(
            flops=2 * tok * ff * feat, bytes_accessed=2 * ff * feat + 2 * tok * feat, transcendentals=tok * feat
        ),
    )(g, w_t)


def add_near_kernel(in_ref, acts_ref, out_ref):
    wide = in_ref.shape[2]
    feat = wide - LANES
    codes, top = encode(decoded_sum(in_ref))
    for k in range(Z16):
        out_ref[k, :, :feat] = codes[2 * k : 2 * k + 2]
        out_ref[k, :, feat:wide] = top[2 * k : 2 * k + 2]
        out_ref[k, :, wide:] = acts_ref[...]


def add_near(parts, acts):
    places, rows, wide = parts.shape
    return pl.pallas_call(
        add_near_kernel,
        out_shape=jax.ShapeDtypeStruct((Z16, rows // Z16, wide + acts.shape[1]), BF16),
        compiler_params=pltpu.CompilerParams(vmem_limit_bytes=16 * 2**20),
        cost_estimate=pl.CostEstimate(flops=10 * parts.size, bytes_accessed=2 * parts.size, transcendentals=parts.size),
    )(parts, acts)


def spread_kernel(in_ref, out_ref, held_ref):
    feat = out_ref.shape[2]
    for k in range(Z16):
        held_ref[2 * k : 2 * k + 2, :] = in_ref[k, :, in_ref.shape[2] - feat :]
    for j in range(Y * Z0):
        out_ref[j] = held_ref[...]


def spread(parts, feat):
    places, rows, _ = parts.shape
    return pl.pallas_call(
        spread_kernel,
        out_shape=jax.ShapeDtypeStruct((Y * Z0, places * rows, feat), BF16),
        scratch_shapes=[pltpu.VMEM((places * rows, feat), BF16)],
        compiler_params=pltpu.CompilerParams(vmem_limit_bytes=16 * 2**20),
        cost_estimate=pl.CostEstimate(flops=0, bytes_accessed=20 * places * rows * feat, transcendentals=0),
    )(parts)


def add_far_kernel(in_ref, out_ref):
    feat = out_ref.shape[1]
    total = decode(in_ref[0, :, :feat], in_ref[0, :, feat : feat + LANES])
    for k in range(1, Z16):
        total = total + decode(in_ref[k, :, :feat], in_ref[k, :, feat : feat + LANES])
    out_ref[...] = total.astype(BF16)


def add_far(parts, feat):
    places, rows, wide = parts.shape
    return pl.pallas_call(
        add_far_kernel,
        out_shape=jax.ShapeDtypeStruct((rows, feat), BF16),
        compiler_params=pltpu.CompilerParams(vmem_limit_bytes=16 * 2**20),
        cost_estimate=pl.CostEstimate(flops=10 * parts.size, bytes_accessed=2 * parts.size, transcendentals=parts.size),
    )(parts)


def ordered(shape, axis):
    tok = shape[0]
    at = lax.broadcasted_iota(jnp.int32, shape, axis)
    token = lax.broadcasted_iota(jnp.int32, shape, 1 - axis)
    rows = tok // (Y * Z0)
    place, rest = at // rows, at % rows
    source = place // Z0 * (rows * Z0) + (rest // 2 * Z0 + place % Z0) * 2 + rest % 2
    return jnp.where(token == source, 1.0, 0.0).astype(BF16)


def weight_kernel(g_ref, act_ref, out_ref, toks_ref):
    tok, ff = g_ref.shape
    chunk = tok // Y

    @pl.when(pl.program_id(0) == 0)
    def _():
        g = requant(g_ref[...].astype(F32).reshape(tok // MXB, MXB, ff), 1).reshape(tok, ff).astype(BF16)
        toks_ref[...] = dot(g, ordered((tok, tok), 1), ((0,), (0,))).astype(BF16)

    width = act_ref.shape[1]
    acts = []
    for y in range(Y):
        a = act_ref[y * chunk : (y + 1) * chunk, :].astype(F32).reshape(Z0, chunk // MXB, MXB // Z0, width)
        halves = [requant(a[:, b].reshape(MXB, width), 0).reshape(Z0, MXB // Z0, width) for b in range(chunk // MXB)]
        acts.append(jnp.stack(halves, axis=1).reshape(chunk, width).astype(BF16))
    out_ref[...] = dot(toks_ref[...], jnp.concatenate(acts, axis=0), ((1,), (0,))).astype(BF16)


def weight_grad(g, acts):
    tok, ff = g.shape
    feat = acts.shape[1]
    tile = feat // TILES
    return pl.pallas_call(
        weight_kernel,
        out_shape=jax.ShapeDtypeStruct((ff, feat), BF16),
        grid=(TILES,),
        in_specs=[pl.BlockSpec((tok, ff), lambda i: (0, 0)), pl.BlockSpec((tok, tile), lambda i: (0, i))],
        out_specs=pl.BlockSpec((ff, tile), lambda i: (0, i)),
        scratch_shapes=[pltpu.VMEM((ff, tok), BF16)],
        compiler_params=pltpu.CompilerParams(vmem_limit_bytes=32 * 2**20),
        cost_estimate=pl.CostEstimate(
            flops=2 * tok * ff * feat + 20 * tok * feat,
            bytes_accessed=2 * ff * feat + 2 * tok * feat,
            transcendentals=0,
        ),
    )(g, acts)


def local(grad_out, acts, weight):
    own, ff = grad_out.shape
    feat = acts.shape[1]
    row, near, far = ("x", "core"), ("y", "z0"), ("zh", "zm")
    copies = jnp.broadcast_to(grad_out[None], (8, own, ff))
    g = lax.all_to_all(copies, row, 0, 0).reshape(8 * own, ff)
    sums = lax.all_to_all(partial_sums(g, weight.T), near, 0, 0)
    parts = lax.all_to_all(add_near(sums, acts), far, 0, 0)
    all_acts = lax.all_to_all(spread(parts, feat), near, 0, 0)
    grad_weight_t = weight_grad(g, all_acts.reshape(-1, feat))
    return add_far(parts, feat), grad_weight_t.T


def solution(mesh):
    fine = Mesh(mesh.devices.reshape(4, 2, Y, ZH, ZM, Z0), ("x", "core", "y", "zh", "zm", "z0"))
    row, col = ("x", "core"), ("y", "zh", "zm", "z0")
    return jax.shard_map(
        local,
        mesh=fine,
        in_specs=(P(row, col), P(col, row), P(row, col)),
        out_specs=(P(col, row), P(row, col)),
        check_vma=False,
    )
```

```python
import jax
import jax.numpy as jnp
from jax import lax
from jax.experimental import pallas as pl
from jax.experimental.pallas import tpu as pltpu
from jax.sharding import Mesh
from jax.sharding import PartitionSpec as P

MXB = 32
CODE_LIMIT = 448.0
PEAK_FLOOR = 0.25
Y, ZH, ZM, Z0 = 4, 8, 2, 2
ZL = ZM * Z0
Z16 = ZH * ZM
LANES = 128
TILES = 4
SPAN = 125.0
F32 = jnp.float32
BF16 = jnp.bfloat16


def block_scale(peaks):
    scale = jnp.full_like(peaks, 2.0 ** (-10))
    for power in range(-1, 8):
        scale = jnp.where(peaks >= 2.0**power, 2.0 ** (power - 8), scale)
    return scale


def requant(blocks, axis):
    peaks = jnp.maximum(jnp.max(jnp.abs(blocks), axis=axis, keepdims=True), PEAK_FLOOR)
    scale = block_scale(peaks)
    limit = CODE_LIMIT * scale
    held = jnp.minimum(jnp.maximum(blocks, -limit), limit) * (1.0 + 2.0**-12)
    wide = held * (2.0**20 + 1.0)
    normal = wide - (wide - held)
    anchor = (1.5 * 2.0**14) * scale
    small = (held + anchor) - anchor
    return jnp.where(jnp.abs(blocks) < 2.0**-6 * scale, small, normal)


def dot(a, b, dims):
    return lax.dot_general(a, b, (dims, ((), ())), preferred_element_type=F32)


def top_of(magnitude):
    return (jnp.maximum(magnitude, 2.0**-90) * (1.0 + 2.0**-7)).astype(BF16)


def encode_with(values, top):
    level = jnp.exp2(jnp.abs(values) * ((2.0 * SPAN) / top.astype(F32)) - SPAN)
    return jnp.where(values < 0.0, -level, level).astype(BF16)


def encode(values):
    top = top_of(jnp.max(jnp.abs(values), axis=1, keepdims=True))
    return encode_with(values, top), jnp.broadcast_to(top, (values.shape[0], LANES))


def decode(codes, top):
    code = codes.astype(F32)
    step = top[:, :1].astype(F32) * (1.0 / (2.0 * SPAN))
    magnitude = (jnp.log2(jnp.abs(code)) + SPAN) * step
    return jnp.where(code < 0.0, -magnitude, magnitude)


def decoded_sum(in_ref):
    feat = in_ref.shape[2] - LANES
    total = decode(in_ref[0, :, :feat], in_ref[0, :, feat:])
    for k in range(1, in_ref.shape[0]):
        total = total + decode(in_ref[k, :, :feat], in_ref[k, :, feat:])
    return total


def partial_kernel(g_ref, w_ref, out_ref, sums_ref):
    tok, ff = g_ref.shape
    feat = w_ref.shape[1]
    tile = feat // TILES
    tiles = [slice(t * tile, (t + 1) * tile) for t in range(TILES)]
    g_t = g_ref[...].astype(F32).T
    codes_t = requant(g_t.reshape(ff // MXB, MXB, tok), 1).reshape(ff, tok).astype(BF16)
    rows = tok // (Y * Z0)
    held = dot(ordered((tok, tok), 0), codes_t, ((1,), (1,))).astype(BF16)
    most = jnp.zeros((tok, LANES), F32)
    for c in tiles:
        part = dot(held, w_ref[:, c], ((1,), (0,)))
        sums_ref[:, c] = part
        for k in range(tile // LANES):
            most = jnp.maximum(most, jnp.abs(part[:, k * LANES : (k + 1) * LANES]))
    top = top_of(jnp.max(most, axis=1, keepdims=True))
    wide = jnp.broadcast_to(top, (tok, LANES))
    for k in range(Y * Z0):
        r = slice(k * rows, (k + 1) * rows)
        out_ref[k, :, :feat] = encode_with(sums_ref[r, :], top[r])
        out_ref[k, :, feat:] = wide[r]


def partial_sums(g, w_t):
    tok, ff = g.shape
    feat = w_t.shape[1]
    return pl.pallas_call(
        partial_kernel,
        out_shape=jax.ShapeDtypeStruct((Y * Z0, tok // (Y * Z0), feat + LANES), BF16),
        scratch_shapes=[pltpu.VMEM((tok, feat), F32)],
        compiler_params=pltpu.CompilerParams(vmem_limit_bytes=16 * 2**20),
        cost_estimate=pl.CostEstimate(
            flops=2 * tok * ff * feat, bytes_accessed=2 * ff * feat + 2 * tok * feat, transcendentals=tok * feat
        ),
    )(g, w_t)


def add_near_kernel(in_ref, acts_ref, out_ref):
    wide = in_ref.shape[2]
    feat = wide - LANES
    codes, top = encode(decoded_sum(in_ref))
    for k in range(Z16):
        out_ref[k, :, :feat] = codes[2 * k : 2 * k + 2]
        out_ref[k, :, feat:wide] = top[2 * k : 2 * k + 2]
        out_ref[k, :, wide:] = acts_ref[...]


def add_near(parts, acts):
    places, rows, wide = parts.shape
    return pl.pallas_call(
        add_near_kernel,
        out_shape=jax.ShapeDtypeStruct((Z16, rows // Z16, wide + acts.shape[1]), BF16),
        compiler_params=pltpu.CompilerParams(vmem_limit_bytes=16 * 2**20),
        cost_estimate=pl.CostEstimate(flops=10 * parts.size, bytes_accessed=2 * parts.size, transcendentals=parts.size),
    )(parts, acts)


def spread_kernel(in_ref, out_ref, held_ref):
    feat = out_ref.shape[2]
    for k in range(Z16):
        held_ref[2 * k : 2 * k + 2, :] = in_ref[k, :, in_ref.shape[2] - feat :]
    for j in range(Y * Z0):
        out_ref[j] = held_ref[...]


def spread(parts, feat):
    places, rows, _ = parts.shape
    return pl.pallas_call(
        spread_kernel,
        out_shape=jax.ShapeDtypeStruct((Y * Z0, places * rows, feat), BF16),
        scratch_shapes=[pltpu.VMEM((places * rows, feat), BF16)],
        compiler_params=pltpu.CompilerParams(vmem_limit_bytes=16 * 2**20),
        cost_estimate=pl.CostEstimate(flops=0, bytes_accessed=20 * places * rows * feat, transcendentals=0),
    )(parts)


def add_far_kernel(in_ref, out_ref):
    feat = out_ref.shape[1]
    total = decode(in_ref[0, :, :feat], in_ref[0, :, feat : feat + LANES])
    for k in range(1, Z16):
        total = total + decode(in_ref[k, :, :feat], in_ref[k, :, feat : feat + LANES])
    out_ref[...] = total.astype(BF16)


def add_far(parts, feat):
    places, rows, wide = parts.shape
    return pl.pallas_call(
        add_far_kernel,
        out_shape=jax.ShapeDtypeStruct((rows, feat), BF16),
        compiler_params=pltpu.CompilerParams(vmem_limit_bytes=16 * 2**20),
        cost_estimate=pl.CostEstimate(flops=10 * parts.size, bytes_accessed=2 * parts.size, transcendentals=parts.size),
    )(parts)


def ordered(shape, axis):
    tok = shape[0]
    at = lax.broadcasted_iota(jnp.int32, shape, axis)
    token = lax.broadcasted_iota(jnp.int32, shape, 1 - axis)
    rows = tok // (Y * Z0)
    place, rest = at // rows, at % rows
    source = place // Z0 * (rows * Z0) + (rest // 2 * Z0 + place % Z0) * 2 + rest % 2
    return jnp.where(token == source, 1.0, 0.0).astype(BF16)


def toks_kernel(g_ref, out_ref):
    tok, ff = g_ref.shape
    g = requant(g_ref[...].astype(F32).reshape(tok // MXB, MXB, ff), 1).reshape(tok, ff).astype(BF16)
    out_ref[...] = dot(g, ordered((tok, tok), 1), ((0,), (0,))).astype(BF16)


def grad_toks(g):
    tok, ff = g.shape
    return pl.pallas_call(
        toks_kernel,
        out_shape=jax.ShapeDtypeStruct((ff, tok), BF16),
        compiler_params=pltpu.CompilerParams(vmem_limit_bytes=16 * 2**20),
        cost_estimate=pl.CostEstimate(flops=2 * tok * tok * ff, bytes_accessed=4 * tok * ff, transcendentals=0),
    )(g)


def weight_kernel(toks_ref, act_ref, out_ref):
    tok, width = act_ref.shape
    chunk = tok // Y
    acts = []
    for y in range(Y):
        a = act_ref[y * chunk : (y + 1) * chunk, :].astype(F32).reshape(Z0, chunk // MXB, MXB // Z0, width)
        halves = [requant(a[:, b].reshape(MXB, width), 0).reshape(Z0, MXB // Z0, width) for b in range(chunk // MXB)]
        acts.append(jnp.stack(halves, axis=1).reshape(chunk, width).astype(BF16))
    out_ref[...] = dot(toks_ref[...], jnp.concatenate(acts, axis=0), ((1,), (0,))).astype(BF16)


def weight_grad(toks, acts):
    ff, tok = toks.shape
    feat = acts.shape[1]
    tile = feat // TILES
    return pl.pallas_call(
        weight_kernel,
        out_shape=jax.ShapeDtypeStruct((ff, feat), BF16),
        grid=(TILES,),
        in_specs=[pl.BlockSpec((ff, tok), lambda i: (0, 0)), pl.BlockSpec((tok, tile), lambda i: (0, i))],
        out_specs=pl.BlockSpec((ff, tile), lambda i: (0, i)),
        compiler_params=pltpu.CompilerParams(vmem_limit_bytes=32 * 2**20),
        cost_estimate=pl.CostEstimate(
            flops=2 * tok * ff * feat + 20 * tok * feat,
            bytes_accessed=2 * ff * feat + 2 * tok * feat,
            transcendentals=0,
        ),
    )(toks, acts)


def local(grad_out, acts, weight):
    own, ff = grad_out.shape
    feat = acts.shape[1]
    row, near, far = ("x", "core"), ("y", "z0"), ("zh", "zm")
    copies = jnp.broadcast_to(grad_out[None], (8, own, ff))
    g = lax.all_to_all(copies, row, 0, 0).reshape(8 * own, ff)
    sums = lax.all_to_all(partial_sums(g, weight.T), near, 0, 0)
    parts = lax.all_to_all(add_near(sums, acts), far, 0, 0)
    all_acts = lax.all_to_all(spread(parts, feat), near, 0, 0)
    grad_weight_t = weight_grad(grad_toks(g), all_acts.reshape(-1, feat))
    return add_far(parts, feat), grad_weight_t.T


def solution(mesh):
    fine = Mesh(mesh.devices.reshape(4, 2, Y, ZH, ZM, Z0), ("x", "core", "y", "zh", "zm", "z0"))
    row, col = ("x", "core"), ("y", "zh", "zm", "z0")
    return jax.shard_map(
        local,
        mesh=fine,
        in_specs=(P(row, col), P(col, row), P(row, col)),
        out_specs=(P(col, row), P(row, col)),
        check_vma=False,
    )
```

```python
import jax
import jax.numpy as jnp
from jax import lax
from jax.experimental import pallas as pl
from jax.experimental.pallas import tpu as pltpu
from jax.sharding import Mesh
from jax.sharding import PartitionSpec as P

MXB = 32
CODE_LIMIT = 448.0
PEAK_FLOOR = 0.25
Y, ZH, ZM, Z0 = 4, 8, 2, 2
ZL = ZM * Z0
Z16 = ZH * ZM
LANES = 128
TILES = 4
SPAN = 125.0
F32 = jnp.float32
BF16 = jnp.bfloat16


def block_scale(peaks):
    scale = jnp.full_like(peaks, 2.0 ** (-10))
    for power in range(-1, 8):
        scale = jnp.where(peaks >= 2.0**power, 2.0 ** (power - 8), scale)
    return scale


def requant(blocks, axis):
    peaks = jnp.maximum(jnp.max(jnp.abs(blocks), axis=axis, keepdims=True), PEAK_FLOOR)
    scale = block_scale(peaks)
    limit = CODE_LIMIT * scale
    held = jnp.minimum(jnp.maximum(blocks, -limit), limit) * (1.0 + 2.0**-12)
    wide = held * (2.0**20 + 1.0)
    normal = wide - (wide - held)
    anchor = (1.5 * 2.0**14) * scale
    small = (held + anchor) - anchor
    return jnp.where(jnp.abs(blocks) < 2.0**-6 * scale, small, normal)


def dot(a, b, dims):
    return lax.dot_general(a, b, (dims, ((), ())), preferred_element_type=F32)


def top_of(magnitude):
    return (jnp.maximum(magnitude, 2.0**-90) * (1.0 + 2.0**-7)).astype(BF16)


def encode_with(values, top):
    level = jnp.exp2(jnp.abs(values) * ((2.0 * SPAN) / top.astype(F32)) - SPAN)
    return jnp.where(values < 0.0, -level, level).astype(BF16)


def encode(values):
    top = top_of(jnp.max(jnp.abs(values), axis=1, keepdims=True))
    return encode_with(values, top), jnp.broadcast_to(top, (values.shape[0], LANES))


def decode(codes, top):
    code = codes.astype(F32)
    step = top[:, :1].astype(F32) * (1.0 / (2.0 * SPAN))
    magnitude = (jnp.log2(jnp.abs(code)) + SPAN) * step
    return jnp.where(code < 0.0, -magnitude, magnitude)


def decoded_sum(in_ref):
    feat = in_ref.shape[2] - LANES
    total = decode(in_ref[0, :, :feat], in_ref[0, :, feat:])
    for k in range(1, in_ref.shape[0]):
        total = total + decode(in_ref[k, :, :feat], in_ref[k, :, feat:])
    return total


def partial_kernel(g_ref, w_ref, out_ref, sums_ref):
    tok, ff = g_ref.shape
    feat = w_ref.shape[1]
    tile = feat // TILES
    tiles = [slice(t * tile, (t + 1) * tile) for t in range(TILES)]
    g_t = g_ref[...].astype(F32).T
    codes_t = requant(g_t.reshape(ff // MXB, MXB, tok), 1).reshape(ff, tok).astype(BF16)
    rows = tok // (Y * Z0)
    held = dot(ordered((tok, tok), 0), codes_t, ((1,), (1,))).astype(BF16)
    most = jnp.zeros((tok, LANES), F32)
    for c in tiles:
        part = dot(held, w_ref[:, c], ((1,), (0,)))
        sums_ref[:, c] = part
        for k in range(tile // LANES):
            most = jnp.maximum(most, jnp.abs(part[:, k * LANES : (k + 1) * LANES]))
    top = top_of(jnp.max(most, axis=1, keepdims=True))
    wide = jnp.broadcast_to(top, (tok, LANES))
    for k in range(Y * Z0):
        r = slice(k * rows, (k + 1) * rows)
        out_ref[k, :, :feat] = encode_with(sums_ref[r, :], top[r])
        out_ref[k, :, feat:] = wide[r]


def fetch_kernel(w_hbm, out_ref, sem):
    copy = pltpu.make_async_copy(w_hbm, out_ref, sem)
    copy.start()
    copy.wait()


def fetch(w_t):
    return pl.pallas_call(
        fetch_kernel,
        out_shape=jax.ShapeDtypeStruct(w_t.shape, w_t.dtype),
        in_specs=[pl.BlockSpec(memory_space=pltpu.HBM)],
        out_specs=pl.BlockSpec(memory_space=pltpu.VMEM),
        scratch_shapes=[pltpu.SemaphoreType.DMA],
        compiler_params=pltpu.CompilerParams(vmem_limit_bytes=16 * 2**20),
        cost_estimate=pl.CostEstimate(flops=0, bytes_accessed=4 * w_t.size, transcendentals=0),
    )(w_t)


def partial_sums(g, w_t):
    tok, ff = g.shape
    feat = w_t.shape[1]
    return pl.pallas_call(
        partial_kernel,
        out_shape=jax.ShapeDtypeStruct((Y * Z0, tok // (Y * Z0), feat + LANES), BF16),
        scratch_shapes=[pltpu.VMEM((tok, feat), F32)],
        compiler_params=pltpu.CompilerParams(vmem_limit_bytes=16 * 2**20),
        cost_estimate=pl.CostEstimate(
            flops=2 * tok * ff * feat, bytes_accessed=2 * ff * feat + 2 * tok * feat, transcendentals=tok * feat
        ),
    )(g, w_t)


def add_near_kernel(in_ref, acts_ref, out_ref):
    wide = in_ref.shape[2]
    feat = wide - LANES
    codes, top = encode(decoded_sum(in_ref))
    for k in range(Z16):
        out_ref[k, :, :feat] = codes[2 * k : 2 * k + 2]
        out_ref[k, :, feat:wide] = top[2 * k : 2 * k + 2]
        out_ref[k, :, wide:] = acts_ref[...]


def add_near(parts, acts):
    places, rows, wide = parts.shape
    return pl.pallas_call(
        add_near_kernel,
        out_shape=jax.ShapeDtypeStruct((Z16, rows // Z16, wide + acts.shape[1]), BF16),
        compiler_params=pltpu.CompilerParams(vmem_limit_bytes=16 * 2**20),
        cost_estimate=pl.CostEstimate(flops=10 * parts.size, bytes_accessed=2 * parts.size, transcendentals=parts.size),
    )(parts, acts)


def spread_kernel(in_ref, out_ref, held_ref):
    feat = out_ref.shape[2]
    for k in range(Z16):
        held_ref[2 * k : 2 * k + 2, :] = in_ref[k, :, in_ref.shape[2] - feat :]
    for j in range(Y * Z0):
        out_ref[j] = held_ref[...]


def spread(parts, feat):
    places, rows, _ = parts.shape
    return pl.pallas_call(
        spread_kernel,
        out_shape=jax.ShapeDtypeStruct((Y * Z0, places * rows, feat), BF16),
        scratch_shapes=[pltpu.VMEM((places * rows, feat), BF16)],
        compiler_params=pltpu.CompilerParams(vmem_limit_bytes=16 * 2**20),
        cost_estimate=pl.CostEstimate(flops=0, bytes_accessed=20 * places * rows * feat, transcendentals=0),
    )(parts)


def add_far_kernel(in_ref, out_ref):
    feat = out_ref.shape[1]
    total = decode(in_ref[0, :, :feat], in_ref[0, :, feat : feat + LANES])
    for k in range(1, Z16):
        total = total + decode(in_ref[k, :, :feat], in_ref[k, :, feat : feat + LANES])
    out_ref[...] = total.astype(BF16)


def add_far(parts, feat):
    places, rows, wide = parts.shape
    return pl.pallas_call(
        add_far_kernel,
        out_shape=jax.ShapeDtypeStruct((rows, feat), BF16),
        compiler_params=pltpu.CompilerParams(vmem_limit_bytes=16 * 2**20),
        cost_estimate=pl.CostEstimate(flops=10 * parts.size, bytes_accessed=2 * parts.size, transcendentals=parts.size),
    )(parts)


def ordered(shape, axis):
    tok = shape[0]
    at = lax.broadcasted_iota(jnp.int32, shape, axis)
    token = lax.broadcasted_iota(jnp.int32, shape, 1 - axis)
    rows = tok // (Y * Z0)
    place, rest = at // rows, at % rows
    source = place // Z0 * (rows * Z0) + (rest // 2 * Z0 + place % Z0) * 2 + rest % 2
    return jnp.where(token == source, 1.0, 0.0).astype(BF16)


def toks_kernel(g_ref, out_ref):
    tok, ff = g_ref.shape
    g = requant(g_ref[...].astype(F32).reshape(tok // MXB, MXB, ff), 1).reshape(tok, ff).astype(BF16)
    out_ref[...] = dot(g, ordered((tok, tok), 1), ((0,), (0,))).astype(BF16)


def grad_toks(g):
    tok, ff = g.shape
    return pl.pallas_call(
        toks_kernel,
        out_shape=jax.ShapeDtypeStruct((ff, tok), BF16),
        compiler_params=pltpu.CompilerParams(vmem_limit_bytes=16 * 2**20),
        cost_estimate=pl.CostEstimate(flops=2 * tok * tok * ff, bytes_accessed=4 * tok * ff, transcendentals=0),
    )(g)


def weight_kernel(toks_ref, act_ref, out_ref):
    tok, width = act_ref.shape
    chunk = tok // Y
    acts = []
    for y in range(Y):
        a = act_ref[y * chunk : (y + 1) * chunk, :].astype(F32).reshape(Z0, chunk // MXB, MXB // Z0, width)
        halves = [requant(a[:, b].reshape(MXB, width), 0).reshape(Z0, MXB // Z0, width) for b in range(chunk // MXB)]
        acts.append(jnp.stack(halves, axis=1).reshape(chunk, width).astype(BF16))
    out_ref[...] = dot(toks_ref[...], jnp.concatenate(acts, axis=0), ((1,), (0,))).astype(BF16)


def weight_grad(toks, acts):
    ff, tok = toks.shape
    feat = acts.shape[1]
    tile = feat // 2
    return pl.pallas_call(
        weight_kernel,
        out_shape=jax.ShapeDtypeStruct((ff, feat), BF16),
        grid=(2,),
        in_specs=[pl.BlockSpec((ff, tok), lambda i: (0, 0)), pl.BlockSpec((tok, tile), lambda i: (0, i))],
        out_specs=pl.BlockSpec((ff, tile), lambda i: (0, i)),
        compiler_params=pltpu.CompilerParams(vmem_limit_bytes=32 * 2**20),
        cost_estimate=pl.CostEstimate(
            flops=2 * tok * ff * feat + 20 * tok * feat,
            bytes_accessed=2 * ff * feat + 2 * tok * feat,
            transcendentals=0,
        ),
    )(toks, acts)


def local(grad_out, acts, weight):
    own, ff = grad_out.shape
    feat = acts.shape[1]
    row, near, far = ("x", "core"), ("y", "z0"), ("zh", "zm")
    copies = jnp.broadcast_to(grad_out[None], (8, own, ff))
    g = lax.all_to_all(copies, row, 0, 0).reshape(8 * own, ff)
    sums = lax.all_to_all(partial_sums(g, fetch(weight.T)), near, 0, 0)
    parts = lax.all_to_all(add_near(sums, acts), far, 0, 0)
    all_acts = lax.all_to_all(spread(parts, feat), near, 0, 0)
    grad_weight_t = weight_grad(grad_toks(g), all_acts.reshape(-1, feat))
    return add_far(parts, feat), grad_weight_t.T


def solution(mesh):
    fine = Mesh(mesh.devices.reshape(4, 2, Y, ZH, ZM, Z0), ("x", "core", "y", "zh", "zm", "z0"))
    row, col = ("x", "core"), ("y", "zh", "zm", "z0")
    return jax.shard_map(
        local,
        mesh=fine,
        in_specs=(P(row, col), P(col, row), P(row, col)),
        out_specs=(P(col, row), P(row, col)),
        check_vma=False,
    )
```

```python
import jax
import jax.numpy as jnp
from jax import lax
from jax.experimental import pallas as pl
from jax.experimental.pallas import tpu as pltpu
from jax.sharding import Mesh
from jax.sharding import PartitionSpec as P

MXB = 32
CODE_LIMIT = 448.0
PEAK_FLOOR = 0.25
Y, ZH, ZM, Z0 = 4, 8, 2, 2
ZL = ZM * Z0
Z16 = ZH * ZM
LANES = 128
TILES = 4
SPAN = 125.0
F32 = jnp.float32
BF16 = jnp.bfloat16


def block_scale(peaks):
    scale = jnp.full_like(peaks, 2.0 ** (-10))
    for power in range(-1, 8):
        scale = jnp.where(peaks >= 2.0**power, 2.0 ** (power - 8), scale)
    return scale


def requant(blocks, axis):
    peaks = jnp.maximum(jnp.max(jnp.abs(blocks), axis=axis, keepdims=True), PEAK_FLOOR)
    scale = block_scale(peaks)
    limit = CODE_LIMIT * scale
    held = jnp.minimum(jnp.maximum(blocks, -limit), limit) * (1.0 + 2.0**-12)
    wide = held * (2.0**20 + 1.0)
    normal = wide - (wide - held)
    anchor = (1.5 * 2.0**14) * scale
    small = (held + anchor) - anchor
    return jnp.where(jnp.abs(blocks) < 2.0**-6 * scale, small, normal)


def dot(a, b, dims):
    return lax.dot_general(a, b, (dims, ((), ())), preferred_element_type=F32)


def top_of(magnitude):
    return (jnp.maximum(magnitude, 2.0**-90) * (1.0 + 2.0**-7)).astype(BF16)


def encode_with(values, top):
    level = jnp.exp2(jnp.abs(values) * ((2.0 * SPAN) / top.astype(F32)) - SPAN)
    return jnp.where(values < 0.0, -level, level)


def encode(values):
    top = top_of(jnp.max(jnp.abs(values), axis=1, keepdims=True))
    return encode_with(values, top), jnp.broadcast_to(top.astype(F32), (values.shape[0], LANES))


def decode(codes, top):
    code = codes.astype(F32)
    step = top[:, :1].astype(F32) * (1.0 / (2.0 * SPAN))
    magnitude = (jnp.log2(jnp.abs(code)) + SPAN) * step
    return jnp.where(code < 0.0, -magnitude, magnitude)


def decoded_sum(in_ref):
    feat = in_ref.shape[2] - LANES
    total = decode(in_ref[0, :, :feat], in_ref[0, :, feat:])
    for k in range(1, in_ref.shape[0]):
        total = total + decode(in_ref[k, :, :feat], in_ref[k, :, feat:])
    return total


def partial_kernel(g_ref, w_ref, out_ref, sums_ref):
    tok, ff = g_ref.shape
    feat = w_ref.shape[1]
    tile = feat // TILES
    tiles = [slice(t * tile, (t + 1) * tile) for t in range(TILES)]
    g_t = g_ref[...].astype(F32).T
    codes_t = requant(g_t.reshape(ff // MXB, MXB, tok), 1).reshape(ff, tok).astype(BF16)
    rows = tok // (Y * Z0)
    held = dot(ordered((tok, tok), 0), codes_t, ((1,), (1,))).astype(BF16)
    most = jnp.zeros((tok, LANES), F32)
    for c in tiles:
        part = dot(held, w_ref[:, c], ((1,), (0,)))
        sums_ref[:, c] = part
        for k in range(tile // LANES):
            most = jnp.maximum(most, jnp.abs(part[:, k * LANES : (k + 1) * LANES]))
    top = top_of(jnp.max(most, axis=1, keepdims=True))
    wide = jnp.broadcast_to(top, (tok, LANES))
    for k in range(Y * Z0):
        r = slice(k * rows, (k + 1) * rows)
        out_ref[k, :, :feat] = encode_with(sums_ref[r, :], top[r]).astype(BF16)
        out_ref[k, :, feat:] = wide[r]


def fetch_kernel(w_hbm, out_ref, sem):
    copy = pltpu.make_async_copy(w_hbm, out_ref, sem)
    copy.start()
    copy.wait()


def fetch(w_t):
    return pl.pallas_call(
        fetch_kernel,
        out_shape=jax.ShapeDtypeStruct(w_t.shape, w_t.dtype),
        in_specs=[pl.BlockSpec(memory_space=pltpu.HBM)],
        out_specs=pl.BlockSpec(memory_space=pltpu.VMEM),
        scratch_shapes=[pltpu.SemaphoreType.DMA],
        compiler_params=pltpu.CompilerParams(vmem_limit_bytes=16 * 2**20),
        cost_estimate=pl.CostEstimate(flops=0, bytes_accessed=4 * w_t.size, transcendentals=0),
    )(w_t)


def partial_sums(g, w_t):
    tok, ff = g.shape
    feat = w_t.shape[1]
    return pl.pallas_call(
        partial_kernel,
        out_shape=jax.ShapeDtypeStruct((Y * Z0, tok // (Y * Z0), feat + LANES), BF16),
        scratch_shapes=[pltpu.VMEM((tok, feat), F32)],
        compiler_params=pltpu.CompilerParams(vmem_limit_bytes=16 * 2**20),
        cost_estimate=pl.CostEstimate(
            flops=2 * tok * ff * feat, bytes_accessed=2 * ff * feat + 2 * tok * feat, transcendentals=tok * feat
        ),
    )(g, w_t)


def add_near_kernel(in_ref, acts_ref, out_ref):
    wide = in_ref.shape[2]
    feat = wide - LANES
    codes, top = encode(decoded_sum(in_ref))
    for k in range(Z16):
        out_ref[k, :, :feat] = codes[2 * k : 2 * k + 2].astype(BF16)
        out_ref[k, :, feat:wide] = top[2 * k : 2 * k + 2].astype(BF16)
        out_ref[k, :, wide:] = acts_ref[...]


def add_near(parts, acts):
    places, rows, wide = parts.shape
    return pl.pallas_call(
        add_near_kernel,
        out_shape=jax.ShapeDtypeStruct((Z16, rows // Z16, wide + acts.shape[1]), BF16),
        compiler_params=pltpu.CompilerParams(vmem_limit_bytes=16 * 2**20),
        cost_estimate=pl.CostEstimate(flops=10 * parts.size, bytes_accessed=2 * parts.size, transcendentals=parts.size),
    )(parts, acts)


def spread_kernel(in_ref, out_ref):
    feat = out_ref.shape[2]
    held = [in_ref[k, :, in_ref.shape[2] - feat :].astype(F32) for k in range(Z16)]
    held = jnp.concatenate(held, axis=0).astype(BF16)
    for j in range(Y * Z0):
        out_ref[j] = held


def spread(parts, feat):
    places, rows, _ = parts.shape
    return pl.pallas_call(
        spread_kernel,
        out_shape=jax.ShapeDtypeStruct((Y * Z0, places * rows, feat), BF16),
        compiler_params=pltpu.CompilerParams(vmem_limit_bytes=16 * 2**20),
        cost_estimate=pl.CostEstimate(flops=0, bytes_accessed=20 * places * rows * feat, transcendentals=0),
    )(parts)


def add_far_kernel(in_ref, out_ref):
    feat = out_ref.shape[1]
    total = decode(in_ref[0, :, :feat], in_ref[0, :, feat : feat + LANES])
    for k in range(1, Z16):
        total = total + decode(in_ref[k, :, :feat], in_ref[k, :, feat : feat + LANES])
    out_ref[...] = total.astype(BF16)


def add_far(parts, feat):
    places, rows, wide = parts.shape
    return pl.pallas_call(
        add_far_kernel,
        out_shape=jax.ShapeDtypeStruct((rows, feat), BF16),
        compiler_params=pltpu.CompilerParams(vmem_limit_bytes=16 * 2**20),
        cost_estimate=pl.CostEstimate(flops=10 * parts.size, bytes_accessed=2 * parts.size, transcendentals=parts.size),
    )(parts)


def ordered(shape, axis):
    tok = shape[0]
    at = lax.broadcasted_iota(jnp.int32, shape, axis)
    token = lax.broadcasted_iota(jnp.int32, shape, 1 - axis)
    rows = tok // (Y * Z0)
    place, rest = at // rows, at % rows
    source = place // Z0 * (rows * Z0) + (rest // 2 * Z0 + place % Z0) * 2 + rest % 2
    return jnp.where(token == source, 1.0, 0.0).astype(BF16)


def toks_kernel(g_ref, out_ref):
    tok, ff = g_ref.shape
    g = requant(g_ref[...].astype(F32).reshape(tok // MXB, MXB, ff), 1).reshape(tok, ff).astype(BF16)
    out_ref[...] = dot(g, ordered((tok, tok), 1), ((0,), (0,))).astype(BF16)


def grad_toks(g):
    tok, ff = g.shape
    return pl.pallas_call(
        toks_kernel,
        out_shape=jax.ShapeDtypeStruct((ff, tok), BF16),
        compiler_params=pltpu.CompilerParams(vmem_limit_bytes=16 * 2**20),
        cost_estimate=pl.CostEstimate(flops=2 * tok * tok * ff, bytes_accessed=4 * tok * ff, transcendentals=0),
    )(g)


def weight_kernel(toks_ref, act_ref, out_ref):
    tok, width = act_ref.shape
    chunk = tok // Y
    acts = []
    for y in range(Y):
        a = act_ref[y * chunk : (y + 1) * chunk, :].astype(F32).reshape(Z0, chunk // MXB, MXB // Z0, width)
        halves = [requant(a[:, b].reshape(MXB, width), 0).reshape(Z0, MXB // Z0, width) for b in range(chunk // MXB)]
        acts.append(jnp.stack(halves, axis=1).reshape(chunk, width).astype(BF16))
    out_ref[...] = dot(toks_ref[...], jnp.concatenate(acts, axis=0), ((1,), (0,))).astype(BF16)


def weight_grad(toks, acts):
    ff, tok = toks.shape
    feat = acts.shape[1]
    tile = feat // 2
    return pl.pallas_call(
        weight_kernel,
        out_shape=jax.ShapeDtypeStruct((ff, feat), BF16),
        grid=(2,),
        in_specs=[pl.BlockSpec((ff, tok), lambda i: (0, 0)), pl.BlockSpec((tok, tile), lambda i: (0, i))],
        out_specs=pl.BlockSpec((ff, tile), lambda i: (0, i)),
        compiler_params=pltpu.CompilerParams(vmem_limit_bytes=32 * 2**20),
        cost_estimate=pl.CostEstimate(
            flops=2 * tok * ff * feat + 20 * tok * feat,
            bytes_accessed=2 * ff * feat + 2 * tok * feat,
            transcendentals=0,
        ),
    )(toks, acts)


def local(grad_out, acts, weight):
    own, ff = grad_out.shape
    feat = acts.shape[1]
    row, near, far = ("x", "core"), ("y", "z0"), ("zh", "zm")
    copies = jnp.broadcast_to(grad_out[None], (8, own, ff))
    g = lax.all_to_all(copies, row, 0, 0).reshape(8 * own, ff)
    sums = lax.all_to_all(partial_sums(g, fetch(weight.T)), near, 0, 0)
    parts = lax.all_to_all(add_near(sums, acts), far, 0, 0)
    all_acts = lax.all_to_all(spread(parts, feat), near, 0, 0)
    grad_weight_t = weight_grad(grad_toks(g), all_acts.reshape(-1, feat))
    return add_far(parts, feat), grad_weight_t.T


def solution(mesh):
    fine = Mesh(mesh.devices.reshape(4, 2, Y, ZH, ZM, Z0), ("x", "core", "y", "zh", "zm", "z0"))
    row, col = ("x", "core"), ("y", "zh", "zm", "z0")
    return jax.shard_map(
        local,
        mesh=fine,
        in_specs=(P(row, col), P(col, row), P(row, col)),
        out_specs=(P(col, row), P(row, col)),
        check_vma=False,
    )
```

```python
import jax
import jax.numpy as jnp
from jax import lax
from jax.experimental import pallas as pl
from jax.experimental.pallas import tpu as pltpu
from jax.sharding import Mesh
from jax.sharding import PartitionSpec as P

MXB = 32
CODE_LIMIT = 448.0
PEAK_FLOOR = 0.25
Y, ZH, ZM, Z0 = 4, 8, 2, 2
ZL = ZM * Z0
Z16 = ZH * ZM
LANES = 128
TILES = 4
SPAN = 125.0
F32 = jnp.float32
BF16 = jnp.bfloat16


def block_scale(peaks):
    scale = jnp.full_like(peaks, 2.0 ** (-10))
    for power in range(-1, 8):
        scale = jnp.where(peaks >= 2.0**power, 2.0 ** (power - 8), scale)
    return scale


def requant(blocks, axis):
    peaks = jnp.maximum(jnp.max(jnp.abs(blocks), axis=axis, keepdims=True), PEAK_FLOOR)
    scale = block_scale(peaks)
    limit = CODE_LIMIT * scale
    held = jnp.minimum(jnp.maximum(blocks, -limit), limit) * (1.0 + 2.0**-12)
    wide = held * (2.0**20 + 1.0)
    normal = wide - (wide - held)
    anchor = (1.5 * 2.0**14) * scale
    small = (held + anchor) - anchor
    return jnp.where(jnp.abs(blocks) < 2.0**-6 * scale, small, normal)


def dot(a, b, dims):
    return lax.dot_general(a, b, (dims, ((), ())), preferred_element_type=F32)


def top_of(magnitude):
    return (jnp.maximum(magnitude, 2.0**-90) * (1.0 + 2.0**-7)).astype(BF16)


def encode_with(values, top):
    level = jnp.exp2(jnp.abs(values) * ((2.0 * SPAN) / top.astype(F32)) - SPAN)
    return jnp.where(values < 0.0, -level, level)


def encode(values):
    top = top_of(jnp.max(jnp.abs(values), axis=1, keepdims=True))
    return encode_with(values, top), jnp.broadcast_to(top.astype(F32), (values.shape[0], LANES))


def decode(codes, top):
    code = codes.astype(F32)
    step = top[:, :1].astype(F32) * (1.0 / (2.0 * SPAN))
    magnitude = (jnp.log2(jnp.abs(code)) + SPAN) * step
    return jnp.where(code < 0.0, -magnitude, magnitude)


def decoded_sum(in_ref):
    feat = in_ref.shape[2] - LANES
    total = decode(in_ref[0, :, :feat], in_ref[0, :, feat:])
    for k in range(1, in_ref.shape[0]):
        total = total + decode(in_ref[k, :, :feat], in_ref[k, :, feat:])
    return total


def partial_kernel(g_ref, w_ref, out_ref, sums_ref):
    tok, ff = g_ref.shape
    feat = w_ref.shape[1]
    tile = feat // TILES
    tiles = [slice(t * tile, (t + 1) * tile) for t in range(TILES)]
    g_t = g_ref[...].astype(F32).T
    codes_t = requant(g_t.reshape(ff // MXB, MXB, tok), 1).reshape(ff, tok).astype(BF16)
    rows = tok // (Y * Z0)
    held = dot(ordered((tok, tok), 0), codes_t, ((1,), (1,))).astype(BF16)
    most = jnp.zeros((tok, LANES), F32)
    for c in tiles:
        part = dot(held, w_ref[:, c], ((1,), (0,)))
        sums_ref[:, c] = part
        for k in range(tile // LANES):
            most = jnp.maximum(most, jnp.abs(part[:, k * LANES : (k + 1) * LANES]))
    top = top_of(jnp.max(most, axis=1, keepdims=True))
    wide = jnp.broadcast_to(top, (tok, LANES))
    for k in range(Y * Z0):
        r = slice(k * rows, (k + 1) * rows)
        out_ref[k, :, :feat] = encode_with(sums_ref[r, :], top[r]).astype(BF16)
        out_ref[k, :, feat:] = wide[r]


def fetch_kernel(w_hbm, out_ref, sem):
    copy = pltpu.make_async_copy(w_hbm, out_ref, sem)
    copy.start()
    copy.wait()


def fetch(w_t):
    return pl.pallas_call(
        fetch_kernel,
        out_shape=jax.ShapeDtypeStruct(w_t.shape, w_t.dtype),
        in_specs=[pl.BlockSpec(memory_space=pltpu.HBM)],
        out_specs=pl.BlockSpec(memory_space=pltpu.VMEM),
        scratch_shapes=[pltpu.SemaphoreType.DMA],
        compiler_params=pltpu.CompilerParams(vmem_limit_bytes=16 * 2**20),
        cost_estimate=pl.CostEstimate(flops=0, bytes_accessed=4 * w_t.size, transcendentals=0),
    )(w_t)


def partial_sums(g, w_t):
    tok, ff = g.shape
    feat = w_t.shape[1]
    return pl.pallas_call(
        partial_kernel,
        out_shape=jax.ShapeDtypeStruct((Y * Z0, tok // (Y * Z0), feat + LANES), BF16),
        scratch_shapes=[pltpu.VMEM((tok, feat), F32)],
        compiler_params=pltpu.CompilerParams(vmem_limit_bytes=16 * 2**20),
        cost_estimate=pl.CostEstimate(
            flops=2 * tok * ff * feat, bytes_accessed=2 * ff * feat + 2 * tok * feat, transcendentals=tok * feat
        ),
    )(g, w_t)


def add_near_kernel(in_ref, acts_ref, out_ref):
    wide = in_ref.shape[2]
    feat = wide - LANES
    codes, top = encode(decoded_sum(in_ref))
    for k in range(Z16):
        out_ref[k, :, :feat] = codes[2 * k : 2 * k + 2].astype(BF16)
        out_ref[k, :, feat:wide] = top[2 * k : 2 * k + 2].astype(BF16)
        out_ref[k, :, wide:] = acts_ref[...]


def add_near(parts, acts):
    places, rows, wide = parts.shape
    return pl.pallas_call(
        add_near_kernel,
        out_shape=jax.ShapeDtypeStruct((Z16, rows // Z16, wide + acts.shape[1]), BF16),
        compiler_params=pltpu.CompilerParams(vmem_limit_bytes=16 * 2**20),
        cost_estimate=pl.CostEstimate(flops=10 * parts.size, bytes_accessed=2 * parts.size, transcendentals=parts.size),
    )(parts, acts)


def send_copies(held_ref, out_ref, sems):
    copies = [pltpu.make_async_copy(held_ref, out_ref.at[j], sems.at[j]) for j in range(out_ref.shape[0])]
    for copy in copies:
        copy.start()
    for copy in copies:
        copy.wait()


def repeat(x, times):
    return pl.pallas_call(
        send_copies,
        out_shape=jax.ShapeDtypeStruct((times,) + x.shape, x.dtype),
        in_specs=[pl.BlockSpec(memory_space=pltpu.VMEM)],
        out_specs=pl.BlockSpec(memory_space=pl.ANY),
        scratch_shapes=[pltpu.SemaphoreType.DMA((times,))],
        compiler_params=pltpu.CompilerParams(vmem_limit_bytes=16 * 2**20),
        cost_estimate=pl.CostEstimate(flops=0, bytes_accessed=2 * times * x.size, transcendentals=0),
    )(x)


def spread_kernel(in_ref, out_ref, held_ref, sems):
    feat = out_ref.shape[2]
    held = [in_ref[k, :, in_ref.shape[2] - feat :].astype(F32) for k in range(Z16)]
    held_ref[...] = jnp.concatenate(held, axis=0).astype(BF16)
    send_copies(held_ref, out_ref, sems)


def spread(parts, feat):
    places, rows, _ = parts.shape
    return pl.pallas_call(
        spread_kernel,
        out_shape=jax.ShapeDtypeStruct((Y * Z0, places * rows, feat), BF16),
        in_specs=[pl.BlockSpec(memory_space=pltpu.VMEM)],
        out_specs=pl.BlockSpec(memory_space=pl.ANY),
        scratch_shapes=[pltpu.VMEM((places * rows, feat), BF16), pltpu.SemaphoreType.DMA((Y * Z0,))],
        compiler_params=pltpu.CompilerParams(vmem_limit_bytes=16 * 2**20),
        cost_estimate=pl.CostEstimate(flops=0, bytes_accessed=20 * places * rows * feat, transcendentals=0),
    )(parts)


def add_far_kernel(in_ref, out_ref):
    feat = out_ref.shape[1]
    total = decode(in_ref[0, :, :feat], in_ref[0, :, feat : feat + LANES])
    for k in range(1, Z16):
        total = total + decode(in_ref[k, :, :feat], in_ref[k, :, feat : feat + LANES])
    out_ref[...] = total.astype(BF16)


def add_far(parts, feat):
    places, rows, wide = parts.shape
    return pl.pallas_call(
        add_far_kernel,
        out_shape=jax.ShapeDtypeStruct((rows, feat), BF16),
        compiler_params=pltpu.CompilerParams(vmem_limit_bytes=16 * 2**20),
        cost_estimate=pl.CostEstimate(flops=10 * parts.size, bytes_accessed=2 * parts.size, transcendentals=parts.size),
    )(parts)


def ordered(shape, axis):
    tok = shape[0]
    at = lax.broadcasted_iota(jnp.int32, shape, axis)
    token = lax.broadcasted_iota(jnp.int32, shape, 1 - axis)
    rows = tok // (Y * Z0)
    place, rest = at // rows, at % rows
    source = place // Z0 * (rows * Z0) + (rest // 2 * Z0 + place % Z0) * 2 + rest % 2
    return jnp.where(token == source, 1.0, 0.0).astype(BF16)


def toks_kernel(g_ref, out_ref):
    tok, ff = g_ref.shape
    g = requant(g_ref[...].astype(F32).reshape(tok // MXB, MXB, ff), 1).reshape(tok, ff).astype(BF16)
    out_ref[...] = dot(g, ordered((tok, tok), 1), ((0,), (0,))).astype(BF16)


def grad_toks(g):
    tok, ff = g.shape
    return pl.pallas_call(
        toks_kernel,
        out_shape=jax.ShapeDtypeStruct((ff, tok), BF16),
        compiler_params=pltpu.CompilerParams(vmem_limit_bytes=16 * 2**20),
        cost_estimate=pl.CostEstimate(flops=2 * tok * tok * ff, bytes_accessed=4 * tok * ff, transcendentals=0),
    )(g)


def weight_kernel(toks_ref, act_ref, out_ref):
    tok, width = act_ref.shape
    chunk = tok // Y
    acts = []
    for y in range(Y):
        a = act_ref[y * chunk : (y + 1) * chunk, :].astype(F32).reshape(Z0, chunk // MXB, MXB // Z0, width)
        halves = [requant(a[:, b].reshape(MXB, width), 0).reshape(Z0, MXB // Z0, width) for b in range(chunk // MXB)]
        acts.append(jnp.stack(halves, axis=1).reshape(chunk, width).astype(BF16))
    out_ref[...] = dot(toks_ref[...], jnp.concatenate(acts, axis=0), ((1,), (0,))).astype(BF16)


def weight_grad(toks, acts):
    ff, tok = toks.shape
    feat = acts.shape[1]
    tile = feat // 2
    return pl.pallas_call(
        weight_kernel,
        out_shape=jax.ShapeDtypeStruct((ff, feat), BF16),
        grid=(2,),
        in_specs=[pl.BlockSpec((ff, tok), lambda i: (0, 0)), pl.BlockSpec((tok, tile), lambda i: (0, i))],
        out_specs=pl.BlockSpec((ff, tile), lambda i: (0, i)),
        compiler_params=pltpu.CompilerParams(vmem_limit_bytes=32 * 2**20),
        cost_estimate=pl.CostEstimate(
            flops=2 * tok * ff * feat + 20 * tok * feat,
            bytes_accessed=2 * ff * feat + 2 * tok * feat,
            transcendentals=0,
        ),
    )(toks, acts)


def local(grad_out, acts, weight):
    own, ff = grad_out.shape
    feat = acts.shape[1]
    row, near, far = ("x", "core"), ("y", "z0"), ("zh", "zm")
    g = lax.all_to_all(repeat(grad_out, 8), row, 0, 0).reshape(8 * own, ff)
    sums = lax.all_to_all(partial_sums(g, fetch(weight.T)), near, 0, 0)
    parts = lax.all_to_all(add_near(sums, acts), far, 0, 0)
    all_acts = lax.all_to_all(spread(parts, feat), near, 0, 0)
    grad_weight_t = weight_grad(grad_toks(g), all_acts.reshape(-1, feat))
    return add_far(parts, feat), grad_weight_t.T


def solution(mesh):
    fine = Mesh(mesh.devices.reshape(4, 2, Y, ZH, ZM, Z0), ("x", "core", "y", "zh", "zm", "z0"))
    row, col = ("x", "core"), ("y", "zh", "zm", "z0")
    return jax.shard_map(
        local,
        mesh=fine,
        in_specs=(P(row, col), P(col, row), P(row, col)),
        out_specs=(P(col, row), P(row, col)),
        check_vma=False,
    )
```
